32 devices in a mesh: cfg: 2 (over y), tm: 4 (over z), col: 2 (over x), mom: 2 (over core).
Axes of the slice: x: 2, y: 2, z: 4, core: 2. Of those that a mesh axis runs over, the one named last changes fastest.
Arguments:
- prop_src: bfloat16 [8, 2, 2, 512, 512], P(('cfg', 'tm'), None, None, None, 'col'), parts along dimension 0, may hold values from -6 to 6
- prop_sink: bfloat16 [8, 2, 512, 512], P(('cfg', 'tm'), None, None, 'col'), parts along dimension 0, may hold values from -0.1875 to 0.1875
- elemental: bfloat16 [8, 2, 2, 128, 128], P(('cfg', 'tm')), parts along dimension 0, may hold values from -0.375 to 0.375
- op_mom: int32 [8], P('mom'), may hold values from 0 to 1
- op_gamma: int32 [8], P('mom'), may hold values from 0 to 15
Outputs:
- three_point: bfloat16 [8, 2, 8, 2, 512, 512], P(('cfg', 'tm'), None, 'mom', None, None, 'col'), parts along dimension 0
The draws below stay inside these ranges and needn't reach their ends.
There are 2 independent parts, one for each index of `cfg`. The reference program is written for one: setup_inputs(seed, part) draws one part's arguments, and reference() takes and returns one part's arrays. A program takes and returns all parts, laid end to end along the dimension named above; an argument that names none is the same for every part. Nothing has to cross between parts.
All inputs are finite; a program needn't handle non-finite values.
Results may differ from the reference program's by a relative error of at most 0.005.
Values may be sent and summed in bfloat16 or wider, within the bound.
No kernel may reach another device: no remote copies, remote signals or barrier semaphores. Data moves between devices by JAX's collectives and lax.ppermute only.
A program may use at most 64 MiB of HBM per device.

```python
import jax
import jax.numpy as jnp
import numpy as np
from jax import lax

NEV = 128
TPD = 1
STOPS = 2
NMOM = 2
W = 512
TIMES = 4
REACH = 2
NOPS = 8


def place_ends(drawn, stream_key, low, high):
    extent = drawn.shape
    index_at = [jax.random.randint(jax.random.fold_in(stream_key, axis), (), 0, extent[axis]) for axis in range(len(extent))]
    drawn = drawn.at[tuple(index_at)].set(low)
    longest = extent.index(max(extent))
    index_at[longest] = (index_at[longest] + 1) % extent[longest]
    return drawn.at[tuple(index_at)].set(high)


def shard_levels(stream_key, shape, cuts, low, high):
    gain, own = 1.0, jax.random.fold_in(stream_key, 6)
    for dim, parts in cuts:
        draws = jnp.exp(jax.random.uniform(jax.random.fold_in(own, dim), (parts,), jnp.float32, low / len(cuts), high / len(cuts)))
        gain = gain * jnp.repeat(draws, shape[dim] // parts).reshape([-1 if axis == dim else 1 for axis in range(len(shape))])
    return gain


def scatter_about(stream_key, extent, scale, most, cuts=(), kind=jnp.bfloat16):
    loudness = shard_levels(stream_key, extent, cuts, -0.22, 0.18) if cuts else 1.0
    result = jax.random.normal(stream_key, extent, jnp.float32) * scale * loudness
    return jnp.minimum(jnp.maximum(result, -most), most).astype(kind)


def setup_inputs(seed: int = 0, part: int = 0) -> dict:
    streams_of = jax.random.split(jax.random.key(seed), 6)
    part_splits = jax.random.split(jax.random.fold_in(streams_of[5], part), 6)
    prop_src = scatter_about(part_splits[0], (TIMES, REACH, 2, W, W), 1.0, 6.0, ((0, 4), (4, 2)))
    prop_sink = scatter_about(part_splits[1], (TIMES, 2, W, W), (2 * W) ** -0.5, 0.1875, ((0, 4), (3, 2)))
    elemental = scatter_about(part_splits[2], (TIMES, NMOM, 2, NEV, NEV), (2 * NEV) ** -0.5, 0.375, ((0, 4),))
    op_mom = place_ends(jax.random.randint(streams_of[3], (NOPS,), 0, NMOM), jax.random.fold_in(streams_of[3], 1), 0, NMOM - 1).astype(jnp.int32)
    op_gamma = place_ends(jax.random.randint(streams_of[4], (NOPS,), 0, 16), jax.random.fold_in(streams_of[4], 1), 0, 15).astype(jnp.int32)
    return dict(prop_src=prop_src, prop_sink=prop_sink, elemental=elemental, op_mom=op_mom, op_gamma=op_gamma)


precise = lax.Precision.HIGHEST


def gamma_tables():
    zero_part = np.zeros((4, 4), dtype=np.float32)
    one_imag = np.array([[0, 0, 0, 1], [0, 0, 1, 0], [0, -1, 0, 0], [-1, 0, 0, 0]], dtype=np.float32)
    two_real = np.array([[0, 0, 0, -1], [0, 0, 1, 0], [0, 1, 0, 0], [-1, 0, 0, 0]], dtype=np.float32)
    three_imag = np.array([[0, 0, 1, 0], [0, 0, 0, -1], [-1, 0, 0, 0], [0, 1, 0, 0]], dtype=np.float32)
    four_real = np.array([[0, 0, 1, 0], [0, 0, 0, 1], [1, 0, 0, 0], [0, 1, 0, 0]], dtype=np.float32)
    factors = ((zero_part, one_imag), (two_real, zero_part), (zero_part, three_imag), (four_real, zero_part))
    reals = []
    imags = []
    for number in range(16):
        left_real = np.eye(4, dtype=np.float32)
        left_imag = np.zeros((4, 4), dtype=np.float32)
        for position, factor in enumerate(factors):
            if (number >> position) & 1:
                new_real = left_real @ factor[0] - left_imag @ factor[1]
                new_imag = left_real @ factor[1] + left_imag @ factor[0]
                left_real, left_imag = new_real, new_imag
        reals.append(left_real)
        imags.append(left_imag)
    return np.stack(reals).astype(np.float32), np.stack(imags).astype(np.float32)


def contract(propagator, elem_pick, gamma_real, gamma_imag, sink_block):
    prop_real = propagator[0].reshape(4, NEV, -1)
    prop_imag = propagator[1].reshape(4, NEV, -1)
    phi_real = elem_pick[:, 0]
    phi_imag = elem_pick[:, 1]
    spin_real = jnp.einsum('oab,sbc->osac', phi_real, prop_real, precision=precise) - jnp.einsum('oab,sbc->osac', phi_imag, prop_imag, precision=precise)
    spin_imag = jnp.einsum('oab,sbc->osac', phi_real, prop_imag, precision=precise) + jnp.einsum('oab,sbc->osac', phi_imag, prop_real, precision=precise)
    mixed_real = jnp.einsum('ost,otac->osac', gamma_real, spin_real, precision=precise) - jnp.einsum('ost,otac->osac', gamma_imag, spin_imag, precision=precise)
    mixed_imag = jnp.einsum('ost,otac->osac', gamma_real, spin_imag, precision=precise) + jnp.einsum('ost,otac->osac', gamma_imag, spin_real, precision=precise)
    count = mixed_real.shape[0]
    mixed_real = lax.optimization_barrier(mixed_real.reshape(count, 4 * NEV, -1).astype(jnp.bfloat16)).astype(jnp.float32)
    mixed_imag = lax.optimization_barrier(mixed_imag.reshape(count, 4 * NEV, -1).astype(jnp.bfloat16)).astype(jnp.float32)
    sink_real = sink_block[0]
    sink_imag = sink_block[1]
    block_real = jnp.einsum('wn,owc->onc', sink_real, mixed_real, precision=precise) + jnp.einsum('wn,owc->onc', sink_imag, mixed_imag, precision=precise)
    block_imag = jnp.einsum('wn,owc->onc', sink_real, mixed_imag, precision=precise) - jnp.einsum('wn,owc->onc', sink_imag, mixed_real, precision=precise)
    return jnp.stack([block_real, block_imag], axis=1).astype(jnp.bfloat16)


def reference(prop_src, prop_sink, elemental, op_mom, op_gamma):
    table_real, table_imag = gamma_tables()
    pick_gamma = (op_gamma[:, None] == jnp.arange(16, dtype=jnp.int32)[None, :]).astype(jnp.float32)
    gamma_real = jnp.einsum('og,gst->ost', pick_gamma, jnp.asarray(table_real, dtype=jnp.float32), precision=precise)
    gamma_imag = jnp.einsum('og,gst->ost', pick_gamma, jnp.asarray(table_imag, dtype=jnp.float32), precision=precise)
    reach_count = STOPS * TPD

    def one_source(source_time):
        own_props = lax.dynamic_index_in_dim(prop_src, source_time, 0, keepdims=False)
        results = []
        for reach_slot in range(reach_count):
            insert_time = ((source_time // TPD + 1 + reach_slot // TPD) * TPD + reach_slot % TPD) % TIMES
            insert_time = insert_time.astype(jnp.int32)
            elem_all = lax.dynamic_index_in_dim(elemental, insert_time, 0, keepdims=False).astype(jnp.float32)
            elem_pick = elem_all[op_mom]
            sink_block = lax.dynamic_index_in_dim(prop_sink, insert_time, 0, keepdims=False).astype(jnp.float32)
            propagator = own_props[reach_slot].astype(jnp.float32)
            results.append(contract(propagator, elem_pick, gamma_real, gamma_imag, sink_block))
        return jnp.stack(results, axis=0)

    return lax.map(one_source, jnp.arange(TIMES, dtype=jnp.int32))
```

```python
import functools

import jax
import jax.numpy as jnp
import numpy as np
from jax import lax
from jax.experimental import pallas as pl
from jax.experimental.pallas import tpu as pltpu
from jax.sharding import PartitionSpec as P

bf16 = jnp.bfloat16
f32 = jnp.float32


def gamma_codes():
    one = np.array([[0, 0, 0, 1j], [0, 0, 1j, 0], [0, -1j, 0, 0], [-1j, 0, 0, 0]])
    two = np.array([[0, 0, 0, -1], [0, 0, 1, 0], [0, 1, 0, 0], [-1, 0, 0, 0]], dtype=complex)
    three = np.array([[0, 0, 1j, 0], [0, 0, 0, -1j], [-1j, 0, 0, 0], [0, 1j, 0, 0]])
    four = np.array([[0, 0, 1, 0], [0, 0, 0, 1], [1, 0, 0, 0], [0, 1, 0, 0]], dtype=complex)
    codes = []
    for number in range(16):
        product = np.eye(4, dtype=complex)
        for position, factor in enumerate((one, two, three, four)):
            if number >> position & 1:
                product = product @ factor
        flip = int(np.nonzero(product[0])[0][0])
        code = flip
        for s in range(4):
            assert np.count_nonzero(product[s]) == 1
            power = [p for p in range(4) if product[s, s ^ flip] == (1, 1j, -1, -1j)[p]]
            code |= power[0] << (2 + 2 * s)
        codes.append(code)
    return codes


CODES = gamma_codes()


def pack_kernel(sink_ref, elem_ref, msg_ref, sink, elem, sems):
    part = lax.axis_index("mom")
    first = pltpu.make_async_copy(sink_ref.at[0, part], sink, sems.at[0])
    first.start()
    moms = elem_ref.shape[1]
    others = [pltpu.make_async_copy(elem_ref.at[0, m, part], elem.at[m], sems.at[1 + m]) for m in range(moms)]
    for copy in others:
        copy.start()
    first.wait()
    columns = sink.shape[1]
    msg_ref[0:columns, :] = sink[...].T
    for m in range(moms):
        others[m].wait()
        for h in range(2):
            msg_ref[columns : columns + 64, (2 * m + h) * 128 : (2 * m + h + 1) * 128] = elem[m, h * 64 : h * 64 + 64, :]


def pack(prop_sink, elemental):
    rows, columns = prop_sink.shape[2:]
    moms, ev = elemental.shape[1], elemental.shape[3]
    return pl.pallas_call(
        pack_kernel,
        out_shape=jax.ShapeDtypeStruct((columns + 64, rows), bf16),
        in_specs=[pl.BlockSpec(memory_space=pl.ANY)] * 2,
        out_specs=pl.BlockSpec(memory_space=pltpu.VMEM),
        scratch_shapes=[
            pltpu.VMEM((rows, columns), bf16),
            pltpu.VMEM((moms, ev, ev), bf16),
            pltpu.SemaphoreType.DMA((1 + moms,)),
        ],
        name="pack",
    )(prop_sink, elemental)


def block_kernel(slot, hop, cols, mom_ref, gamma_ref, mine_ref, other_ref, emine_ref, eother_ref, prop_ref, prev_ref,
                 out_ref, prop, spins, made, prop_sem, out_sems):
    del prev_ref
    width = prop.shape[2]
    part = lax.axis_index("mom")
    source = lax.rem(lax.axis_index("col") + hop, cols)
    fetch = pltpu.make_async_copy(prop_ref.at[0, slot], prop, prop_sem)
    fetch.start()
    fetch.wait()
    moms = spins.shape[0]
    real_first = part == 0

    def elementals(ref, m):
        return jnp.concatenate([ref[:, (2 * m + h) * 128 : (2 * m + h + 1) * 128] for h in range(2)], axis=0)

    lefts = []
    for m in range(moms):
        one, two = elementals(emine_ref, m), elementals(eother_ref, m)
        phi_real = jnp.where(real_first, one, two)
        phi_imag = jnp.where(real_first, two, one)
        lefts.append(jnp.concatenate([phi_real, -phi_imag], axis=1))
        lefts.append(jnp.concatenate([phi_imag, phi_real], axis=1))
    left = jnp.concatenate(lefts, axis=0)
    for s in range(4):
        right = jnp.concatenate([prop[0, s * 128 : s * 128 + 128, :], prop[1, s * 128 : s * 128 + 128, :]], axis=0)
        both = jnp.dot(left, right, preferred_element_type=f32).astype(bf16)
        for m in range(moms):
            real = both[m * 256 : m * 256 + 128]
            imag = both[m * 256 + 128 : m * 256 + 256]
            spins[m, 0, s] = real
            spins[m, 1, s] = -imag
            spins[m, 2, s] = -real
            spins[m, 3, s] = imag

    ops = out_ref.shape[2]
    sinks = jnp.concatenate([mine_ref[...], other_ref[...]], axis=1)

    def copy_out(o, at):
        rows = pl.ds(pl.multiple_of(source * width, width), width)
        return pltpu.make_async_copy(made.at[at], out_ref.at[0, slot, o, :, rows, :], out_sems.at[at])

    @pl.loop(0, ops)
    def _(o):
        at = lax.rem(o, 2)

        @pl.when(o >= 2)
        def _():
            copy_out(o - 2, at).wait()

        number = gamma_ref[o]
        mom = mom_ref[o]
        code = jnp.int32(0)
        for g in range(16):
            code = jnp.where(number == g, jnp.int32(CODES[g]), code)
        flip = code & 3
        for which in range(2):
            pieces = []
            for held in (part, 1 - part):
                turn = 3 * held if which == 0 else 3 - held
                for s in range(4):
                    power = ((code >> (2 + 2 * s)) + turn) & 3
                    pieces.append(spins[mom, power, s ^ flip])
            right = jnp.concatenate(pieces, axis=0)
            made[at, which] = jnp.dot(sinks, right, preferred_element_type=f32).astype(bf16)
        copy_out(o, at).start()

    for o in range(max(ops - 2, 0), ops):
        copy_out(o, o % 2).wait()


def blocks(slot, hop, cols, op_mom, op_gamma, mine, other, emine, eother, prop_src, prev, out_shape):
    width = prop_src.shape[4]
    rows = prop_src.shape[3]
    moms = 2
    ops = out_shape[2]
    any_spec = pl.BlockSpec(memory_space=pl.ANY)
    vmem_spec = pl.BlockSpec(memory_space=pltpu.VMEM)
    smem_spec = pl.BlockSpec(memory_space=pltpu.SMEM)
    operands = [op_mom, op_gamma, mine, other, emine, eother, prop_src]
    specs = [smem_spec] * 2 + [vmem_spec] * 4 + [any_spec]
    body = functools.partial(block_kernel, slot, hop, cols)
    aliases = {}
    if prev is None:
        full = body

        def body(*refs):
            return full(*refs[:7], None, *refs[7:])
    else:
        operands.append(prev)
        specs.append(any_spec)
        aliases = {7: 0}
    return pl.pallas_call(
        body,
        out_shape=jax.ShapeDtypeStruct(out_shape, bf16),
        in_specs=specs,
        out_specs=any_spec,
        input_output_aliases=aliases,
        scratch_shapes=[
            pltpu.VMEM((2, rows, width), bf16),
            pltpu.VMEM((moms, 4, 4, 128, width), bf16),
            pltpu.VMEM((2, 2, width, width), bf16),
            pltpu.SemaphoreType.DMA,
            pltpu.SemaphoreType.DMA((2,)),
        ],
        cost_estimate=pl.CostEstimate(
            flops=2 * ops * 2 * width * 2 * rows * width, bytes_accessed=4 * ops * width * width + 4 * rows * width * 2, transcendentals=0
        ),
        name="blocks",
    )(*operands)


def on_device(prop_src, prop_sink, elemental, op_mom, op_gamma):
    width = prop_src.shape[4]
    rows = prop_src.shape[3]
    stops = prop_src.shape[1]
    ops = op_mom.shape[0]
    cols = lax.axis_size("col")
    times = lax.axis_size("tm")
    later = [((i + 1) % times, i) for i in range(times)]
    swap = [(0, 1), (1, 0)]
    out_shape = (1, stops, ops, 2, rows, width)
    held = pack(prop_sink, elemental)
    out = None
    for slot in range(stops):
        held = lax.ppermute(held, "tm", later)
        other = lax.ppermute(held, "mom", swap)
        emine, eother = held[width:], other[width:]
        for hop in range(cols):
            if hop == 0:
                mine, theirs = held[:width], other[:width]
            else:
                mine = lax.ppermute(held[:width], "col", [((i + hop) % cols, i) for i in range(cols)])
                theirs = lax.ppermute(mine, "mom", swap)
            out = blocks(slot, hop, cols, op_mom, op_gamma, mine, theirs, emine, eother, prop_src, out, out_shape)
    return out


def solution(mesh):
    return jax.shard_map(
        on_device,
        mesh=mesh,
        in_specs=(
            P(("cfg", "tm"), None, None, None, "col"),
            P(("cfg", "tm"), None, None, "col"),
            P(("cfg", "tm"), None, None, None, None),
            P("mom"),
            P("mom"),
        ),
        out_specs=P(("cfg", "tm"), None, "mom", None, None, "col"),
        check_vma=False,
    )
```

```python
import functools

import jax
import jax.numpy as jnp
import numpy as np
from jax import lax
from jax.experimental import pallas as pl
from jax.experimental.pallas import tpu as pltpu
from jax.sharding import PartitionSpec as P

bf16 = jnp.bfloat16
f32 = jnp.float32
LIMIT = 16 * 2**20


def gamma_codes():
    one = np.array([[0, 0, 0, 1j], [0, 0, 1j, 0], [0, -1j, 0, 0], [-1j, 0, 0, 0]])
    two = np.array([[0, 0, 0, -1], [0, 0, 1, 0], [0, 1, 0, 0], [-1, 0, 0, 0]], dtype=complex)
    three = np.array([[0, 0, 1j, 0], [0, 0, 0, -1j], [-1j, 0, 0, 0], [0, 1j, 0, 0]])
    four = np.array([[0, 0, 1, 0], [0, 0, 0, 1], [1, 0, 0, 0], [0, 1, 0, 0]], dtype=complex)
    codes = []
    for number in range(16):
        product = np.eye(4, dtype=complex)
        for position, factor in enumerate((one, two, three, four)):
            if number >> position & 1:
                product = product @ factor
        flip = int(np.nonzero(product[0])[0][0])
        code = flip
        for s in range(4):
            assert np.count_nonzero(product[s]) == 1
            power = [p for p in range(4) if product[s, s ^ flip] == (1, 1j, -1, -1j)[p]]
            code |= power[0] << (2 + 2 * s)
        codes.append(code)
    return codes


CODES = gamma_codes()


def pack_kernel(sink_ref, elem_ref, msg_ref, sink, elem, sems):
    part = lax.axis_index("mom")
    first = pltpu.make_async_copy(sink_ref.at[0, part], sink, sems.at[0])
    first.start()
    moms = elem_ref.shape[1]
    others = [pltpu.make_async_copy(elem_ref.at[0, m, part], elem.at[m], sems.at[1 + m]) for m in range(moms)]
    for copy in others:
        copy.start()
    first.wait()
    columns = sink.shape[1]
    msg_ref[0:columns, :] = sink[...].T
    for m in range(moms):
        others[m].wait()
        for h in range(2):
            msg_ref[columns : columns + 64, (2 * m + h) * 128 : (2 * m + h + 1) * 128] = elem[m, h * 64 : h * 64 + 64, :]


def pack(prop_sink, elemental):
    rows, columns = prop_sink.shape[2:]
    moms, ev = elemental.shape[1], elemental.shape[3]
    return pl.pallas_call(
        pack_kernel,
        out_shape=jax.ShapeDtypeStruct((columns + 64, rows), bf16),
        in_specs=[pl.BlockSpec(memory_space=pl.ANY)] * 2,
        out_specs=pl.BlockSpec(memory_space=pltpu.VMEM),
        scratch_shapes=[
            pltpu.VMEM((rows, columns), bf16),
            pltpu.VMEM((moms, ev, ev), bf16),
            pltpu.SemaphoreType.DMA((1 + moms,)),
        ],
        compiler_params=pltpu.CompilerParams(vmem_limit_bytes=LIMIT),
        name="pack",
    )(prop_sink, elemental)


def spin_kernel(slot, mine_ref, other_ref, prop_ref, spins, prop, prop_sem):
    fetch = pltpu.make_async_copy(prop_ref.at[0, slot], prop, prop_sem)
    fetch.start()
    moms = spins.shape[0]
    width = prop.shape[2]
    real_first = lax.axis_index("mom") == 0

    def elementals(ref, m):
        return jnp.concatenate(
            [ref[width : width + 64, (2 * m + h) * 128 : (2 * m + h + 1) * 128] for h in range(2)], axis=0
        )

    lefts = []
    for m in range(moms):
        one, two = elementals(mine_ref, m), elementals(other_ref, m)
        phi_real = jnp.where(real_first, one, two)
        phi_imag = jnp.where(real_first, two, one)
        lefts.append(jnp.concatenate([phi_real, -phi_imag], axis=1))
        lefts.append(jnp.concatenate([phi_imag, phi_real], axis=1))
    left = jnp.concatenate(lefts, axis=0)
    fetch.wait()
    for s in range(4):
        right = jnp.concatenate([prop[0, s * 128 : s * 128 + 128, :], prop[1, s * 128 : s * 128 + 128, :]], axis=0)
        both = jnp.dot(left, right, preferred_element_type=f32).astype(bf16)
        for m in range(moms):
            real = both[m * 256 : m * 256 + 128]
            imag = both[m * 256 + 128 : m * 256 + 256]
            spins[m, 0, s] = real
            spins[m, 1, s] = -imag
            spins[m, 2, s] = -real
            spins[m, 3, s] = imag


def spin_products(slot, mine, other, prop_src):
    rows, width = prop_src.shape[3:]
    moms = 2
    vmem_spec = pl.BlockSpec(memory_space=pltpu.VMEM)
    return pl.pallas_call(
        functools.partial(spin_kernel, slot),
        out_shape=jax.ShapeDtypeStruct((moms, 4, 4, 128, width), bf16),
        in_specs=[vmem_spec, vmem_spec, pl.BlockSpec(memory_space=pl.ANY)],
        out_specs=vmem_spec,
        scratch_shapes=[pltpu.VMEM((2, rows, width), bf16), pltpu.SemaphoreType.DMA],
        compiler_params=pltpu.CompilerParams(vmem_limit_bytes=LIMIT),
        cost_estimate=pl.CostEstimate(flops=2 * moms * 256 * 256 * 4 * width, bytes_accessed=6 * rows * width * 2, transcendentals=0),
        name="spin_products",
    )(mine, other, prop_src)


def block_kernel(slot, hop, cols, mom_ref, gamma_ref, mine_ref, other_ref, spins, prev_ref, out_ref, made, out_sems):
    del prev_ref
    width = spins.shape[4]
    part = lax.axis_index("mom")
    source = lax.rem(lax.axis_index("col") + hop, cols)
    ops = out_ref.shape[2]
    sinks = jnp.concatenate([mine_ref[0:width, :], other_ref[0:width, :]], axis=1)

    def copy_out(o, which):
        rows = pl.ds(pl.multiple_of(source * width, width), width)
        return pltpu.make_async_copy(made.at[o, which], out_ref.at[0, slot, o, which, rows, :], out_sems.at[o, which])

    @pl.loop(0, ops)
    def _(o):
        number = gamma_ref[o]
        mom = mom_ref[o]
        code = jnp.int32(0)
        for g in range(16):
            code = jnp.where(number == g, jnp.int32(CODES[g]), code)
        flip = code & 3
        for which in range(2):
            pieces = []
            for held in (part, 1 - part):
                turn = 3 * held if which == 0 else 3 - held
                for s in range(4):
                    power = ((code >> (2 + 2 * s)) + turn) & 3
                    pieces.append(spins[mom, power, s ^ flip])
            right = jnp.concatenate(pieces, axis=0)
            made[o, which] = jnp.dot(sinks, right, preferred_element_type=f32).astype(bf16)
            copy_out(o, which).start()

    for o in range(ops):
        for which in range(2):
            copy_out(o, which).wait()


def blocks(slot, hop, cols, op_mom, op_gamma, mine, other, spins, prev, out_shape):
    width = spins.shape[4]
    rows = out_shape[4]
    ops = out_shape[2]
    any_spec = pl.BlockSpec(memory_space=pl.ANY)
    vmem_spec = pl.BlockSpec(memory_space=pltpu.VMEM)
    smem_spec = pl.BlockSpec(memory_space=pltpu.SMEM)
    operands = [op_mom, op_gamma, mine, other, spins]
    specs = [smem_spec] * 2 + [vmem_spec] * 3
    body = functools.partial(block_kernel, slot, hop, cols)
    aliases = {}
    if prev is None:
        full = body

        def body(*refs):
            return full(*refs[:5], None, *refs[5:])
    else:
        operands.append(prev)
        specs.append(any_spec)
        aliases = {5: 0}
    return pl.pallas_call(
        body,
        out_shape=jax.ShapeDtypeStruct(out_shape, bf16),
        in_specs=specs,
        out_specs=any_spec,
        input_output_aliases=aliases,
        scratch_shapes=[
            pltpu.VMEM((ops, 2, width, width), bf16),
            pltpu.SemaphoreType.DMA((ops, 2)),
        ],
        compiler_params=pltpu.CompilerParams(vmem_limit_bytes=LIMIT),
        cost_estimate=pl.CostEstimate(
            flops=2 * ops * 2 * width * 2 * rows * width, bytes_accessed=4 * ops * width * width + 4 * rows * width * 2, transcendentals=0
        ),
        name="blocks",
    )(*operands)


def on_device(prop_src, prop_sink, elemental, op_mom, op_gamma):
    width = prop_src.shape[4]
    rows = prop_src.shape[3]
    stops = prop_src.shape[1]
    ops = op_mom.shape[0]
    cols = lax.axis_size("col")
    times = lax.axis_size("tm")
    later = [((i + 1) % times, i) for i in range(times)]
    swap = [(0, 1), (1, 0)]
    out_shape = (1, stops, ops, 2, rows, width)
    held = pack(prop_sink, elemental)
    out = None
    for slot in range(stops):
        held = lax.ppermute(held, "tm", later)
        other = lax.ppermute(held, "mom", swap)
        spins = spin_products(slot, held, other, prop_src)
        for hop in range(cols):
            if hop == 0:
                mine, theirs = held, other
            else:
                mine = lax.ppermute(held[:width], "col", [((i + hop) % cols, i) for i in range(cols)])
                theirs = lax.ppermute(mine, "mom", swap)
            out = blocks(slot, hop, cols, op_mom, op_gamma, mine, theirs, spins, out, out_shape)
    return out


def solution(mesh):
    return jax.shard_map(
        on_device,
        mesh=mesh,
        in_specs=(
            P(("cfg", "tm"), None, None, None, "col"),
            P(("cfg", "tm"), None, None, "col"),
            P(("cfg", "tm"), None, None, None, None),
            P("mom"),
            P("mom"),
        ),
        out_specs=P(("cfg", "tm"), None, "mom", None, None, "col"),
        check_vma=False,
    )
```

```python
import functools

import jax
import jax.numpy as jnp
import numpy as np
from jax import lax
from jax.experimental import pallas as pl
from jax.experimental.pallas import tpu as pltpu
from jax.sharding import PartitionSpec as P

bf16 = jnp.bfloat16
f32 = jnp.float32
LIMIT = 16 * 2**20


def gamma_codes():
    one = np.array([[0, 0, 0, 1j], [0, 0, 1j, 0], [0, -1j, 0, 0], [-1j, 0, 0, 0]])
    two = np.array([[0, 0, 0, -1], [0, 0, 1, 0], [0, 1, 0, 0], [-1, 0, 0, 0]], dtype=complex)
    three = np.array([[0, 0, 1j, 0], [0, 0, 0, -1j], [-1j, 0, 0, 0], [0, 1j, 0, 0]])
    four = np.array([[0, 0, 1, 0], [0, 0, 0, 1], [1, 0, 0, 0], [0, 1, 0, 0]], dtype=complex)
    codes = []
    for number in range(16):
        product = np.eye(4, dtype=complex)
        for position, factor in enumerate((one, two, three, four)):
            if number >> position & 1:
                product = product @ factor
        flip = int(np.nonzero(product[0])[0][0])
        code = flip
        for s in range(4):
            assert np.count_nonzero(product[s]) == 1
            power = [p for p in range(4) if product[s, s ^ flip] == (1, 1j, -1, -1j)[p]]
            code |= power[0] << (2 + 2 * s)
        codes.append(code)
    return codes


CODES = gamma_codes()


def pack_kernel(sink_ref, elem_ref, msg_ref, sink, elem, sems):
    part = lax.axis_index("mom")
    first = pltpu.make_async_copy(sink_ref.at[0, part], sink, sems.at[0])
    first.start()
    moms = elem_ref.shape[1]
    others = [pltpu.make_async_copy(elem_ref.at[0, m, part], elem.at[m], sems.at[1 + m]) for m in range(moms)]
    for copy in others:
        copy.start()
    first.wait()
    columns = sink.shape[1]
    msg_ref[0:columns, :] = sink[...].T
    for m in range(moms):
        others[m].wait()
        for h in range(2):
            msg_ref[columns : columns + 64, (2 * m + h) * 128 : (2 * m + h + 1) * 128] = elem[m, h * 64 : h * 64 + 64, :]


def pack(prop_sink, elemental):
    rows, columns = prop_sink.shape[2:]
    moms, ev = elemental.shape[1], elemental.shape[3]
    return pl.pallas_call(
        pack_kernel,
        out_shape=jax.ShapeDtypeStruct((columns + 64, rows), bf16),
        in_specs=[pl.BlockSpec(memory_space=pl.ANY)] * 2,
        out_specs=pl.BlockSpec(memory_space=pltpu.VMEM),
        scratch_shapes=[
            pltpu.VMEM((rows, columns), bf16),
            pltpu.VMEM((moms, ev, ev), bf16),
            pltpu.SemaphoreType.DMA((1 + moms,)),
        ],
        compiler_params=pltpu.CompilerParams(vmem_limit_bytes=LIMIT),
        name="pack",
    )(prop_sink, elemental)


def mixed_kernel(slot, mom_ref, gamma_ref, mine_ref, other_ref, prop_ref, mixed, prop, spins, prop_sem):
    fetch = pltpu.make_async_copy(prop_ref.at[0, slot], prop, prop_sem)
    fetch.start()
    moms = spins.shape[0]
    width = prop.shape[2]
    real_first = lax.axis_index("mom") == 0

    def elementals(ref, m):
        return jnp.concatenate(
            [ref[width : width + 64, (2 * m + h) * 128 : (2 * m + h + 1) * 128] for h in range(2)], axis=0
        )

    lefts = []
    for m in range(moms):
        one, two = elementals(mine_ref, m), elementals(other_ref, m)
        phi_real = jnp.where(real_first, one, two)
        phi_imag = jnp.where(real_first, two, one)
        lefts.append(jnp.concatenate([phi_real, -phi_imag], axis=1))
        lefts.append(jnp.concatenate([phi_imag, phi_real], axis=1))
    left = jnp.concatenate(lefts, axis=0)
    fetch.wait()
    for s in range(4):
        right = jnp.concatenate([prop[0, s * 128 : s * 128 + 128, :], prop[1, s * 128 : s * 128 + 128, :]], axis=0)
        both = jnp.dot(left, right, preferred_element_type=f32).astype(bf16)
        for m in range(moms):
            real = both[m * 256 : m * 256 + 128]
            imag = both[m * 256 + 128 : m * 256 + 256]
            spins[m, 0, s] = real
            spins[m, 1, s] = -imag
            spins[m, 2, s] = -real
            spins[m, 3, s] = imag

    @pl.loop(0, mixed.shape[0])
    def _(o):
        number = gamma_ref[o]
        mom = mom_ref[o]
        code = jnp.int32(0)
        for g in range(16):
            code = jnp.where(number == g, jnp.int32(CODES[g]), code)
        flip = code & 3
        for s in range(4):
            power = code >> (2 + 2 * s)
            for form, turn in enumerate((0, 3, 2)):
                mixed[o, form, s * 128 : s * 128 + 128, :] = spins[mom, (power + turn) & 3, s ^ flip]


def mixed_blocks(slot, op_mom, op_gamma, mine, other, prop_src):
    rows, width = prop_src.shape[3:]
    ops = op_mom.shape[0]
    moms = 2
    vmem_spec = pl.BlockSpec(memory_space=pltpu.VMEM)
    smem_spec = pl.BlockSpec(memory_space=pltpu.SMEM)
    return pl.pallas_call(
        functools.partial(mixed_kernel, slot),
        out_shape=jax.ShapeDtypeStruct((ops, 3, rows, width), bf16),
        in_specs=[smem_spec, smem_spec, vmem_spec, vmem_spec, pl.BlockSpec(memory_space=pl.ANY)],
        out_specs=vmem_spec,
        scratch_shapes=[
            pltpu.VMEM((2, rows, width), bf16),
            pltpu.VMEM((moms, 4, 4, 128, width), bf16),
            pltpu.SemaphoreType.DMA,
        ],
        compiler_params=pltpu.CompilerParams(vmem_limit_bytes=LIMIT),
        cost_estimate=pl.CostEstimate(flops=2 * moms * 256 * 256 * 4 * width, bytes_accessed=6 * rows * width * 2, transcendentals=0),
        name="mixed",
    )(op_mom, op_gamma, mine, other, prop_src)


def block_kernel(slot, hop, cols, mine_ref, other_ref, mixed, prev_ref, out_ref, made, out_sems):
    del prev_ref
    ops, width = mixed.shape[0], mixed.shape[3]
    part = lax.axis_index("mom")
    source = lax.rem(lax.axis_index("col") + hop, cols)
    sinks = jnp.concatenate([mine_ref[0:width, :], other_ref[0:width, :]], axis=1)
    rows = pl.ds(pl.multiple_of(source * width, width), width)
    copies = []
    for o in range(ops):
        for which in range(2):
            right = jnp.concatenate([mixed[o, which + part], mixed[o, which + 1 - part]], axis=0)
            made[o, which] = jnp.dot(sinks, right, preferred_element_type=f32).astype(bf16)
            copies.append(
                pltpu.make_async_copy(made.at[o, which], out_ref.at[0, slot, o, which, rows, :], out_sems.at[o, which])
            )
            copies[-1].start()
    for copy in copies:
        copy.wait()


def blocks(slot, hop, cols, mine, other, mixed, prev, out_shape):
    rows, width = out_shape[4:]
    ops = out_shape[2]
    any_spec = pl.BlockSpec(memory_space=pl.ANY)
    vmem_spec = pl.BlockSpec(memory_space=pltpu.VMEM)
    operands = [mine, other, mixed]
    specs = [vmem_spec] * 3
    body = functools.partial(block_kernel, slot, hop, cols)
    aliases = {}
    if prev is None:
        full = body

        def body(*refs):
            return full(*refs[:3], None, *refs[3:])
    else:
        operands.append(prev)
        specs.append(any_spec)
        aliases = {3: 0}
    return pl.pallas_call(
        body,
        out_shape=jax.ShapeDtypeStruct(out_shape, bf16),
        in_specs=specs,
        out_specs=any_spec,
        input_output_aliases=aliases,
        scratch_shapes=[
            pltpu.VMEM((ops, 2, width, width), bf16),
            pltpu.SemaphoreType.DMA((ops, 2)),
        ],
        compiler_params=pltpu.CompilerParams(vmem_limit_bytes=LIMIT),
        cost_estimate=pl.CostEstimate(
            flops=2 * ops * 2 * width * 2 * rows * width, bytes_accessed=4 * ops * width * width + 4 * rows * width * 2, transcendentals=0
        ),
        name="blocks",
    )(*operands)


def on_device(prop_src, prop_sink, elemental, op_mom, op_gamma):
    width = prop_src.shape[4]
    rows = prop_src.shape[3]
    stops = prop_src.shape[1]
    ops = op_mom.shape[0]
    cols = lax.axis_size("col")
    times = lax.axis_size("tm")
    later = [((i + 1) % times, i) for i in range(times)]
    swap = [(0, 1), (1, 0)]
    out_shape = (1, stops, ops, 2, rows, width)
    held = pack(prop_sink, elemental)
    out = None
    waiting = []
    for slot in range(stops):
        held = lax.ppermute(held, "tm", later)
        if out is not None:
            held, out = lax.optimization_barrier((held, out))
        other = lax.ppermute(held, "mom", swap)
        mixed = mixed_blocks(slot, op_mom, op_gamma, held, other, prop_src)
        arrivals = []
        for hop in range(1, cols):
            mine = lax.ppermute(held[:width], "col", [((i + hop) % cols, i) for i in range(cols)])
            arrivals.append((slot, hop, mine, mixed))
        out = blocks(slot, 0, cols, held, other, mixed, out, out_shape)
        for place, hop, mine, theirs, mixes in waiting:
            out = blocks(place, hop, cols, mine, theirs, mixes, out, out_shape)
        waiting = []
        for place, hop, mine, mixes in arrivals:
            if slot == stops - 1:
                mine, out = lax.optimization_barrier((mine, out))
            waiting.append((place, hop, mine, lax.ppermute(mine, "mom", swap), mixes))
    for place, hop, mine, theirs, mixes in waiting:
        out = blocks(place, hop, cols, mine, theirs, mixes, out, out_shape)
    return out


def solution(mesh):
    return jax.shard_map(
        on_device,
        mesh=mesh,
        in_specs=(
            P(("cfg", "tm"), None, None, None, "col"),
            P(("cfg", "tm"), None, None, "col"),
            P(("cfg", "tm"), None, None, None, None),
            P("mom"),
            P("mom"),
        ),
        out_specs=P(("cfg", "tm"), None, "mom", None, None, "col"),
        check_vma=False,
    )
```

```python
import functools

import jax
import jax.numpy as jnp
import numpy as np
from jax import lax
from jax.experimental import pallas as pl
from jax.experimental.pallas import tpu as pltpu
from jax.sharding import PartitionSpec as P

bf16 = jnp.bfloat16
f32 = jnp.float32
LIMIT = 16 * 2**20


def gamma_codes():
    one = np.array([[0, 0, 0, 1j], [0, 0, 1j, 0], [0, -1j, 0, 0], [-1j, 0, 0, 0]])
    two = np.array([[0, 0, 0, -1], [0, 0, 1, 0], [0, 1, 0, 0], [-1, 0, 0, 0]], dtype=complex)
    three = np.array([[0, 0, 1j, 0], [0, 0, 0, -1j], [-1j, 0, 0, 0], [0, 1j, 0, 0]])
    four = np.array([[0, 0, 1, 0], [0, 0, 0, 1], [1, 0, 0, 0], [0, 1, 0, 0]], dtype=complex)
    codes = []
    for number in range(16):
        product = np.eye(4, dtype=complex)
        for position, factor in enumerate((one, two, three, four)):
            if number >> position & 1:
                product = product @ factor
        flip = int(np.nonzero(product[0])[0][0])
        code = flip
        for s in range(4):
            assert np.count_nonzero(product[s]) == 1
            power = [p for p in range(4) if product[s, s ^ flip] == (1, 1j, -1, -1j)[p]]
            code |= power[0] << (2 + 2 * s)
        codes.append(code)
    return codes


CODES = gamma_codes()


def pack_kernel(sink_ref, elem_ref, msg_ref, sink, elem, sems):
    part = lax.axis_index("mom")
    first = pltpu.make_async_copy(sink_ref.at[0, part], sink, sems.at[0])
    first.start()
    moms = elem_ref.shape[1]
    others = [pltpu.make_async_copy(elem_ref.at[0, m, part], elem.at[m], sems.at[1 + m]) for m in range(moms)]
    for copy in others:
        copy.start()
    first.wait()
    columns = sink.shape[1]
    msg_ref[0:columns, :] = sink[...].T
    for m in range(moms):
        others[m].wait()
        for h in range(2):
            msg_ref[columns : columns + 64, (2 * m + h) * 128 : (2 * m + h + 1) * 128] = elem[m, h * 64 : h * 64 + 64, :]


def pack(prop_sink, elemental):
    rows, columns = prop_sink.shape[2:]
    moms, ev = elemental.shape[1], elemental.shape[3]
    return pl.pallas_call(
        pack_kernel,
        out_shape=jax.ShapeDtypeStruct((columns + 64, rows), bf16),
        in_specs=[pl.BlockSpec(memory_space=pltpu.HBM)] * 2,
        out_specs=pl.BlockSpec(memory_space=pltpu.VMEM),
        scratch_shapes=[
            pltpu.VMEM((rows, columns), bf16),
            pltpu.VMEM((moms, ev, ev), bf16),
            pltpu.SemaphoreType.DMA((1 + moms,)),
        ],
        compiler_params=pltpu.CompilerParams(vmem_limit_bytes=LIMIT),
        name="pack",
    )(prop_sink, elemental)


def fetch_kernel(mom_ref, gamma_ref, prop_ref, *refs):
    *props, picks, sems = refs
    copies = [pltpu.make_async_copy(prop_ref.at[0, slot], prop, sems.at[slot]) for slot, prop in enumerate(props)]
    for copy in copies:
        copy.start()
    for o in range(mom_ref.shape[0]):
        code = jnp.int32(0)
        for g in range(16):
            code = jnp.where(gamma_ref[o] == g, jnp.int32(CODES[g]), code)
        picks[0, o] = mom_ref[o]
        picks[1, o] = code
    for copy in copies:
        copy.wait()


def fetch(op_mom, op_gamma, prop_src):
    slots, parts, rows, width = prop_src.shape[1:]
    ops = op_mom.shape[0]
    vmem_spec = pl.BlockSpec(memory_space=pltpu.VMEM)
    smem_spec = pl.BlockSpec(memory_space=pltpu.SMEM)
    return pl.pallas_call(
        fetch_kernel,
        out_shape=[jax.ShapeDtypeStruct((parts, rows, width), bf16)] * slots + [jax.ShapeDtypeStruct((2, ops), jnp.int32)],
        in_specs=[smem_spec, smem_spec, pl.BlockSpec(memory_space=pltpu.HBM)],
        out_specs=[vmem_spec] * slots + [smem_spec],
        scratch_shapes=[pltpu.SemaphoreType.DMA((slots,))],
        compiler_params=pltpu.CompilerParams(vmem_limit_bytes=LIMIT),
        name="fetch",
    )(op_mom, op_gamma, prop_src)


def joined(refs):
    return jnp.concatenate([ref[...] for ref in refs], axis=0)


def mixed_kernel(picks, mine_ref, *refs):
    *others, prop, mixed, spins = refs
    moms = spins.shape[0]
    width = prop.shape[2]
    real_first = lax.axis_index("mom") == 0

    def elementals(rows, m):
        return jnp.concatenate([rows[:, (2 * m + h) * 128 : (2 * m + h + 1) * 128] for h in range(2)], axis=0)

    mine = mine_ref[width : width + 64, :]
    other = joined(others)[width : width + 64, :]

    lefts = []
    for m in range(moms):
        one, two = elementals(mine, m), elementals(other, m)
        phi_real = jnp.where(real_first, one, two)
        phi_imag = jnp.where(real_first, two, one)
        lefts.append(jnp.concatenate([phi_real, -phi_imag], axis=1))
        lefts.append(jnp.concatenate([phi_imag, phi_real], axis=1))
    left = jnp.concatenate(lefts, axis=0)
    for s in range(4):
        right = jnp.concatenate([prop[0, s * 128 : s * 128 + 128, :], prop[1, s * 128 : s * 128 + 128, :]], axis=0)
        both = jnp.dot(left, right, preferred_element_type=f32).astype(bf16)
        for m in range(moms):
            real = both[m * 256 : m * 256 + 128]
            imag = both[m * 256 + 128 : m * 256 + 256]
            spins[m, 0, s] = real
            spins[m, 1, s] = -imag
            spins[m, 2, s] = -real
            spins[m, 3, s] = imag

    @pl.loop(0, mixed.shape[0])
    def _(o):
        mom = picks[0, o]
        code = picks[1, o]
        flip = code & 3
        for s in range(4):
            power = code >> (2 + 2 * s)
            for form, turn in enumerate((0, 3, 2)):
                mixed[o, form, s * 128 : s * 128 + 128, :] = spins[mom, (power + turn) & 3, s ^ flip]


def mixed_blocks(picks, mine, other, prop):
    parts, rows, width = prop.shape
    ops = picks.shape[1]
    moms = 2
    vmem_spec = pl.BlockSpec(memory_space=pltpu.VMEM)
    return pl.pallas_call(
        mixed_kernel,
        out_shape=jax.ShapeDtypeStruct((ops, 3, rows, width), bf16),
        in_specs=[pl.BlockSpec(memory_space=pltpu.SMEM)] + [vmem_spec] * (2 + len(other)),
        out_specs=vmem_spec,
        scratch_shapes=[pltpu.VMEM((moms, 4, 4, 128, width), bf16)],
        compiler_params=pltpu.CompilerParams(vmem_limit_bytes=LIMIT),
        cost_estimate=pl.CostEstimate(flops=1, bytes_accessed=1, transcendentals=0),
        name="mixed",
    )(picks, mine, *other, prop)


def block_kernel(places, cols, counts, *refs):
    groups = []
    for count in counts:
        groups.append(refs[: count + 1])
        refs = refs[count + 1 :]
    mixes = dict(zip(sorted({slot for slot, _ in places}), refs))
    out_ref, made, out_sems = refs[-3:]
    part = lax.axis_index("mom")
    copies = []
    for place, ((slot, hop), (mine, *others)) in enumerate(zip(places, groups)):
        mixed = mixes[slot]
        ops, width = mixed.shape[0], mixed.shape[3]
        source = lax.rem(lax.axis_index("col") + hop, cols)
        sinks = jnp.concatenate([mine[0:width, :], joined(others)[0:width, :]], axis=1)
        rows = pl.ds(pl.multiple_of(source * width, width), width)
        for o in range(ops):
            for which in range(2):
                right = jnp.concatenate([mixed[o, which + part], mixed[o, which + 1 - part]], axis=0)
                made[place, o, which] = jnp.dot(sinks, right, preferred_element_type=f32).astype(bf16)
                copies.append(
                    pltpu.make_async_copy(
                        made.at[place, o, which], out_ref.at[0, slot, o, which, rows, :], out_sems.at[place, o, which]
                    )
                )
                copies[-1].start()
    for copy in copies:
        copy.wait()


def blocks(cols, work, mixes, prev, out_shape):
    rows, width = out_shape[4:]
    ops = out_shape[2]
    any_spec = pl.BlockSpec(memory_space=pl.ANY)
    vmem_spec = pl.BlockSpec(memory_space=pltpu.VMEM)
    places = [(slot, hop) for slot, hop, _, _ in work]
    operands = [ref for _, _, mine, others in work for ref in (mine, *others)]
    operands += [mixes[slot] for slot in sorted({slot for slot, _ in places})]
    specs = [vmem_spec] * len(operands)
    aliases = {}
    if prev is not None:
        aliases = {len(operands): 0}
        operands.append(prev)
        specs.append(any_spec)
    return pl.pallas_call(
        functools.partial(block_kernel, places, cols, [len(others) for _, _, _, others in work]),
        out_shape=jax.ShapeDtypeStruct(out_shape, bf16),
        in_specs=specs,
        out_specs=any_spec,
        input_output_aliases=aliases,
        scratch_shapes=[
            pltpu.VMEM((len(places), ops, 2, width, width), bf16),
            pltpu.SemaphoreType.DMA((len(places), ops, 2)),
        ],
        compiler_params=pltpu.CompilerParams(vmem_limit_bytes=LIMIT),
        cost_estimate=pl.CostEstimate(flops=1, bytes_accessed=1, transcendentals=0),
        name="blocks",
    )(*operands)


def on_device(prop_src, prop_sink, elemental, op_mom, op_gamma):
    width = prop_src.shape[4]
    rows = prop_src.shape[3]
    stops = prop_src.shape[1]
    ops = op_mom.shape[0]
    cols = lax.axis_size("col")
    times = lax.axis_size("tm")
    later = [((i + 1) % times, i) for i in range(times)]
    swap = [(0, 1), (1, 0)]
    out_shape = (1, stops, ops, 2, rows, width)
    def swapped(block, pieces):
        size = block.shape[0] // pieces
        return [lax.ppermute(block[i * size : (i + 1) * size], "mom", swap) for i in range(pieces)]

    held = pack(prop_sink, elemental)
    out = None
    mixes = {}
    waiting = []
    for slot in range(stops):
        held = lax.ppermute(held, "tm", later)
        if slot == 0:
            *props, picks = fetch(op_mom, op_gamma, prop_src)
            held, props, picks = lax.optimization_barrier((held, props, picks))
        else:
            held, out = lax.optimization_barrier((held, out))
        other = swapped(held, 2)
        arrivals = [
            (slot, hop, lax.ppermute(held[:width], "col", [((i + hop) % cols, i) for i in range(cols)]))
            for hop in range(1, cols)
        ]
        mixes[slot] = mixed_blocks(picks, held, other, props[slot])
        out = blocks(cols, waiting + [(slot, 0, held, other)], mixes, out, out_shape)
        waiting = []
        for place, hop, mine in arrivals:
            if slot == stops - 1:
                mine, out = lax.optimization_barrier((mine, out))
            waiting.append((place, hop, mine, swapped(mine, 2)))
    return blocks(cols, waiting, mixes, out, out_shape)


def solution(mesh):
    return jax.shard_map(
        on_device,
        mesh=mesh,
        in_specs=(
            P(("cfg", "tm"), None, None, None, "col"),
            P(("cfg", "tm"), None, None, "col"),
            P(("cfg", "tm"), None, None, None, None),
            P("mom"),
            P("mom"),
        ),
        out_specs=P(("cfg", "tm"), None, "mom", None, None, "col"),
        check_vma=False,
    )
```

```python
import functools

import jax
import jax.numpy as jnp
import numpy as np
from jax import lax
from jax.experimental import pallas as pl
from jax.experimental.pallas import tpu as pltpu
from jax.sharding import PartitionSpec as P

bf16 = jnp.bfloat16
f32 = jnp.float32
LIMIT = 16 * 2**20


def gamma_codes():
    one = np.array([[0, 0, 0, 1j], [0, 0, 1j, 0], [0, -1j, 0, 0], [-1j, 0, 0, 0]])
    two = np.array([[0, 0, 0, -1], [0, 0, 1, 0], [0, 1, 0, 0], [-1, 0, 0, 0]], dtype=complex)
    three = np.array([[0, 0, 1j, 0], [0, 0, 0, -1j], [-1j, 0, 0, 0], [0, 1j, 0, 0]])
    four = np.array([[0, 0, 1, 0], [0, 0, 0, 1], [1, 0, 0, 0], [0, 1, 0, 0]], dtype=complex)
    codes = []
    for number in range(16):
        product = np.eye(4, dtype=complex)
        for position, factor in enumerate((one, two, three, four)):
            if number >> position & 1:
                product = product @ factor
        flip = int(np.nonzero(product[0])[0][0])
        code = flip
        for s in range(4):
            assert np.count_nonzero(product[s]) == 1
            power = [p for p in range(4) if product[s, s ^ flip] == (1, 1j, -1, -1j)[p]]
            code |= power[0] << (2 + 2 * s)
        codes.append(code)
    return codes


CODES = gamma_codes()


def pack_kernel(sink_ref, elem_ref, msg_ref, sink, elem, sems):
    part = lax.axis_index("mom")
    first = pltpu.make_async_copy(sink_ref.at[0, part], sink, sems.at[0])
    first.start()
    moms = elem_ref.shape[1]
    others = [pltpu.make_async_copy(elem_ref.at[0, m, part], elem.at[m], sems.at[1 + m]) for m in range(moms)]
    for copy in others:
        copy.start()
    first.wait()
    columns = sink.shape[1]
    msg_ref[0:columns, :] = sink[...].T
    for m in range(moms):
        others[m].wait()
        for h in range(2):
            msg_ref[columns : columns + 64, (2 * m + h) * 128 : (2 * m + h + 1) * 128] = elem[m, h * 64 : h * 64 + 64, :]


def pack(prop_sink, elemental):
    rows, columns = prop_sink.shape[2:]
    moms, ev = elemental.shape[1], elemental.shape[3]
    return pl.pallas_call(
        pack_kernel,
        out_shape=jax.ShapeDtypeStruct((columns + 64, rows), bf16),
        in_specs=[pl.BlockSpec(memory_space=pltpu.HBM)] * 2,
        out_specs=pl.BlockSpec(memory_space=pltpu.VMEM),
        scratch_shapes=[
            pltpu.VMEM((rows, columns), bf16),
            pltpu.VMEM((moms, ev, ev), bf16),
            pltpu.SemaphoreType.DMA((1 + moms,)),
        ],
        compiler_params=pltpu.CompilerParams(vmem_limit_bytes=LIMIT),
        name="pack",
    )(prop_sink, elemental)


def fetch_kernel(mom_ref, gamma_ref, prop_ref, *refs):
    *props, picks, sems = refs
    copies = [pltpu.make_async_copy(prop_ref.at[0, slot], prop, sems.at[slot]) for slot, prop in enumerate(props)]
    for copy in copies:
        copy.start()
    for o in range(mom_ref.shape[0]):
        code = jnp.int32(0)
        for g in range(16):
            code = jnp.where(gamma_ref[o] == g, jnp.int32(CODES[g]), code)
        picks[0, o] = mom_ref[o]
        picks[1, o] = code
    for copy in copies:
        copy.wait()


def fetch(op_mom, op_gamma, prop_src):
    slots, parts, rows, width = prop_src.shape[1:]
    ops = op_mom.shape[0]
    vmem_spec = pl.BlockSpec(memory_space=pltpu.VMEM)
    smem_spec = pl.BlockSpec(memory_space=pltpu.SMEM)
    return pl.pallas_call(
        fetch_kernel,
        out_shape=[jax.ShapeDtypeStruct((parts, rows, width), bf16)] * slots + [jax.ShapeDtypeStruct((2, ops), jnp.int32)],
        in_specs=[smem_spec, smem_spec, pl.BlockSpec(memory_space=pltpu.HBM)],
        out_specs=[vmem_spec] * slots + [smem_spec],
        scratch_shapes=[pltpu.SemaphoreType.DMA((slots,))],
        compiler_params=pltpu.CompilerParams(vmem_limit_bytes=LIMIT),
        name="fetch",
    )(op_mom, op_gamma, prop_src)


def joined(refs):
    return jnp.concatenate([ref[...] for ref in refs], axis=0)


def mixed_kernel(picks, mine_ref, *refs):
    *others, prop, mixed, spins, chosen, chosen_sem = refs
    fetched = pltpu.make_async_copy(picks, chosen, chosen_sem)
    fetched.start()
    moms = spins.shape[0]
    width = prop.shape[2]
    real_first = lax.axis_index("mom") == 0

    def elementals(rows, m):
        return jnp.concatenate([rows[:, (2 * m + h) * 128 : (2 * m + h + 1) * 128] for h in range(2)], axis=0)

    mine = mine_ref[width : width + 64, :]
    other = joined(others)[width : width + 64, :]

    lefts = []
    for m in range(moms):
        one, two = elementals(mine, m), elementals(other, m)
        phi_real = jnp.where(real_first, one, two)
        phi_imag = jnp.where(real_first, two, one)
        lefts.append(jnp.concatenate([phi_real, -phi_imag], axis=1))
        lefts.append(jnp.concatenate([phi_imag, phi_real], axis=1))
    left = jnp.concatenate(lefts, axis=0)
    for s in range(4):
        right = jnp.concatenate([prop[0, s * 128 : s * 128 + 128, :], prop[1, s * 128 : s * 128 + 128, :]], axis=0)
        both = jnp.dot(left, right, preferred_element_type=f32).astype(bf16)
        for m in range(moms):
            real = both[m * 256 : m * 256 + 128]
            imag = both[m * 256 + 128 : m * 256 + 256]
            spins[m, 0, s] = real
            spins[m, 1, s] = -imag
            spins[m, 2, s] = -real
            spins[m, 3, s] = imag

    fetched.wait()
    for o in range(mixed.shape[0]):
        mom = chosen[0, o]
        code = chosen[1, o]
        flip = code & 3
        for s in range(4):
            power = code >> (2 + 2 * s)
            for form, turn in enumerate((0, 3)):
                mixed[o, form, s * 128 : s * 128 + 128, :] = spins[mom, (power + turn) & 3, s ^ flip]


def mixed_blocks(picks, mine, other, prop):
    parts, rows, width = prop.shape
    ops = picks.shape[1]
    moms = 2
    vmem_spec = pl.BlockSpec(memory_space=pltpu.VMEM)
    return pl.pallas_call(
        mixed_kernel,
        out_shape=jax.ShapeDtypeStruct((ops, 2, rows, width), bf16),
        in_specs=[pl.BlockSpec(memory_space=pl.ANY)] + [vmem_spec] * (2 + len(other)),
        out_specs=vmem_spec,
        scratch_shapes=[
            pltpu.VMEM((moms, 4, 4, 128, width), bf16),
            pltpu.SMEM((2, ops), jnp.int32),
            pltpu.SemaphoreType.DMA,
        ],
        compiler_params=pltpu.CompilerParams(vmem_limit_bytes=LIMIT),
        cost_estimate=pl.CostEstimate(flops=1, bytes_accessed=1, transcendentals=0),
        name="mixed",
    )(picks, mine, *other, prop)


def block_kernel(places, cols, counts, *refs):
    groups = []
    for count in counts:
        groups.append(refs[: count + 1])
        refs = refs[count + 1 :]
    mixes = dict(zip(sorted({slot for slot, _ in places}), refs))
    out_ref, made, out_sems = refs[-3:]
    part = lax.axis_index("mom")
    copies = []
    for place, ((slot, hop), (mine, *others)) in enumerate(zip(places, groups)):
        mixed = mixes[slot]
        ops, width = mixed.shape[0], mixed.shape[3]
        source = lax.rem(lax.axis_index("col") + hop, cols)
        ours, theirs = mine[0:width, :], joined(others)[0:width, :]
        sinks = [
            jnp.concatenate([ours, theirs], axis=1),
            jnp.concatenate([jnp.where(part == 0, ours, -ours), jnp.where(part == 0, -theirs, theirs)], axis=1),
        ]
        rows = pl.ds(pl.multiple_of(source * width, width), width)
        for o in range(ops):
            for which in range(2):
                first = part if which == 0 else 1 - part
                right = jnp.concatenate([mixed[o, first], mixed[o, 1 - first]], axis=0)
                made[place, o, which] = jnp.dot(sinks[which], right, preferred_element_type=f32).astype(bf16)
                copies.append(
                    pltpu.make_async_copy(
                        made.at[place, o, which], out_ref.at[0, slot, o, which, rows, :], out_sems.at[place, o, which]
                    )
                )
                copies[-1].start()
    for copy in copies:
        copy.wait()


def blocks(cols, work, mixes, prev, out_shape):
    rows, width = out_shape[4:]
    ops = out_shape[2]
    any_spec = pl.BlockSpec(memory_space=pl.ANY)
    vmem_spec = pl.BlockSpec(memory_space=pltpu.VMEM)
    places = [(slot, hop) for slot, hop, _, _ in work]
    operands = [ref for _, _, mine, others in work for ref in (mine, *others)]
    operands += [mixes[slot] for slot in sorted({slot for slot, _ in places})]
    specs = [vmem_spec] * len(operands)
    aliases = {}
    if prev is not None:
        aliases = {len(operands): 0}
        operands.append(prev)
        specs.append(any_spec)
    return pl.pallas_call(
        functools.partial(block_kernel, places, cols, [len(others) for _, _, _, others in work]),
        out_shape=jax.ShapeDtypeStruct(out_shape, bf16),
        in_specs=specs,
        out_specs=any_spec,
        input_output_aliases=aliases,
        scratch_shapes=[
            pltpu.VMEM((len(places), ops, 2, width, width), bf16),
            pltpu.SemaphoreType.DMA((len(places), ops, 2)),
        ],
        compiler_params=pltpu.CompilerParams(vmem_limit_bytes=LIMIT),
        cost_estimate=pl.CostEstimate(flops=1, bytes_accessed=1, transcendentals=0),
        name="blocks",
    )(*operands)


def signed(block, negative):
    return jnp.where(negative, -block, block)


def half_kernel(mine_ref, mixed, sums):
    part = lax.axis_index("mom")
    for o in range(sums.shape[0]):
        for which in range(2):
            left = mine_ref[...] if which == 0 else signed(mine_ref[...], part == 1)
            first = part if which == 0 else 1 - part
            sums[o, which] = jnp.dot(left, mixed[o, first], preferred_element_type=f32)


def half(mine, mixed):
    ops, width = mixed.shape[0], mixed.shape[3]
    vmem_spec = pl.BlockSpec(memory_space=pltpu.VMEM)
    return pl.pallas_call(
        half_kernel,
        out_shape=jax.ShapeDtypeStruct((ops, 2, width, width), f32),
        in_specs=[vmem_spec] * 2,
        out_specs=vmem_spec,
        compiler_params=pltpu.CompilerParams(vmem_limit_bytes=LIMIT),
        cost_estimate=pl.CostEstimate(flops=1, bytes_accessed=1, transcendentals=0),
        name="half",
    )(mine, mixed)


def rest_kernel(slot, hop, cols, count, *refs):
    others = refs[:count]
    mixed, sums, _, out_ref, made, out_sems = refs[count:]
    ops, width = mixed.shape[0], mixed.shape[3]
    part = lax.axis_index("mom")
    source = lax.rem(lax.axis_index("col") + hop, cols)
    rows = pl.ds(pl.multiple_of(source * width, width), width)
    theirs = joined(others)
    copies = []
    for o in range(ops):
        for which in range(2):
            left = theirs if which == 0 else signed(theirs, part == 0)
            first = part if which == 0 else 1 - part
            block = sums[o, which] + jnp.dot(left, mixed[o, 1 - first], preferred_element_type=f32)
            made[o, which] = block.astype(bf16)
            copies.append(
                pltpu.make_async_copy(made.at[o, which], out_ref.at[0, slot, o, which, rows, :], out_sems.at[o, which])
            )
            copies[-1].start()
    for copy in copies:
        copy.wait()


def rest(slot, hop, cols, others, mixed, sums, prev):
    ops, width = mixed.shape[0], mixed.shape[3]
    any_spec = pl.BlockSpec(memory_space=pl.ANY)
    vmem_spec = pl.BlockSpec(memory_space=pltpu.VMEM)
    return pl.pallas_call(
        functools.partial(rest_kernel, slot, hop, cols, len(others)),
        out_shape=jax.ShapeDtypeStruct(prev.shape, bf16),
        in_specs=[vmem_spec] * (len(others) + 2) + [any_spec],
        out_specs=any_spec,
        input_output_aliases={len(others) + 2: 0},
        scratch_shapes=[pltpu.VMEM((ops, 2, width, width), bf16), pltpu.SemaphoreType.DMA((ops, 2))],
        compiler_params=pltpu.CompilerParams(vmem_limit_bytes=LIMIT),
        cost_estimate=pl.CostEstimate(flops=1, bytes_accessed=1, transcendentals=0),
        name="rest",
    )(*others, mixed, sums, prev)


def on_device(prop_src, prop_sink, elemental, op_mom, op_gamma):
    width = prop_src.shape[4]
    rows = prop_src.shape[3]
    stops = prop_src.shape[1]
    ops = op_mom.shape[0]
    cols = lax.axis_size("col")
    times = lax.axis_size("tm")
    later = [((i + 1) % times, i) for i in range(times)]
    swap = [(0, 1), (1, 0)]
    out_shape = (1, stops, ops, 2, rows, width)
    def swapped(block, pieces):
        cuts = [0, *(block.shape[0] * p // 20 // 16 * 16 for p in pieces), block.shape[0]]
        return [lax.ppermute(block[i:j], "mom", swap) for i, j in zip(cuts, cuts[1:])]

    held = pack(prop_sink, elemental)
    out = None
    mixes = {}
    waiting = []
    for slot in range(stops):
        held = lax.ppermute(held, "tm", later)
        if slot == 0:
            *props, picks = fetch(op_mom, op_gamma, prop_src)
            held, props, picks = lax.optimization_barrier((held, props, picks))
        else:
            held, out = lax.optimization_barrier((held, out))
        other = swapped(held, (6,) if slot == 0 else (6,))
        arrivals = [
            (slot, hop, lax.ppermute(held[:width], "col", [((i + hop) % cols, i) for i in range(cols)]))
            for hop in range(1, cols)
        ]
        mixes[slot] = mixed_blocks(picks, held, other, props[slot])
        out = blocks(cols, waiting + [(slot, 0, held, other)], mixes, out, out_shape)
        waiting = []
        for place, hop, mine in arrivals:
            if slot == stops - 1:
                mine, out = lax.optimization_barrier((mine, out))
            waiting.append((place, hop, mine, swapped(mine, (5,) if slot == 0 else ())))
    for slot, hop, mine, others in waiting:
        out = rest(slot, hop, cols, others, mixes[slot], half(mine, mixes[slot]), out)
    return out


def solution(mesh):
    return jax.shard_map(
        on_device,
        mesh=mesh,
        in_specs=(
            P(("cfg", "tm"), None, None, None, "col"),
            P(("cfg", "tm"), None, None, "col"),
            P(("cfg", "tm"), None, None, None, None),
            P("mom"),
            P("mom"),
        ),
        out_specs=P(("cfg", "tm"), None, "mom", None, None, "col"),
        check_vma=False,
    )
```

```python
import functools

import jax
import jax.numpy as jnp
import numpy as np
from jax import lax
from jax.experimental import pallas as pl
from jax.experimental.pallas import tpu as pltpu
from jax.sharding import PartitionSpec as P

bf16 = jnp.bfloat16
f32 = jnp.float32
LIMIT = 16 * 2**20


def gamma_codes():
    one = np.array([[0, 0, 0, 1j], [0, 0, 1j, 0], [0, -1j, 0, 0], [-1j, 0, 0, 0]])
    two = np.array([[0, 0, 0, -1], [0, 0, 1, 0], [0, 1, 0, 0], [-1, 0, 0, 0]], dtype=complex)
    three = np.array([[0, 0, 1j, 0], [0, 0, 0, -1j], [-1j, 0, 0, 0], [0, 1j, 0, 0]])
    four = np.array([[0, 0, 1, 0], [0, 0, 0, 1], [1, 0, 0, 0], [0, 1, 0, 0]], dtype=complex)
    codes = []
    for number in range(16):
        product = np.eye(4, dtype=complex)
        for position, factor in enumerate((one, two, three, four)):
            if number >> position & 1:
                product = product @ factor
        flip = int(np.nonzero(product[0])[0][0])
        code = flip
        for s in range(4):
            assert np.count_nonzero(product[s]) == 1
            power = [p for p in range(4) if product[s, s ^ flip] == (1, 1j, -1, -1j)[p]]
            code |= power[0] << (2 + 2 * s)
        codes.append(code)
    return codes


CODES = gamma_codes()


def turn_kernel(sink_ref, message, sink, sem):
    first = pltpu.make_async_copy(sink_ref.at[0, lax.axis_index("mom")], sink, sem)
    first.start()
    first.wait()
    message[...] = sink[...].T


def turned(prop_sink):
    rows, columns = prop_sink.shape[2:]
    return pl.pallas_call(
        turn_kernel,
        out_shape=jax.ShapeDtypeStruct((columns, rows), bf16),
        in_specs=[pl.BlockSpec(memory_space=pl.ANY)],
        out_specs=pl.BlockSpec(memory_space=pltpu.VMEM),
        scratch_shapes=[pltpu.VMEM((rows, columns), bf16), pltpu.SemaphoreType.DMA],
        compiler_params=pltpu.CompilerParams(vmem_limit_bytes=LIMIT),
        name="turned",
    )(prop_sink)


def lay_kernel(after_ref, elem_ref, message, elem, sems):
    del after_ref
    part = lax.axis_index("mom")
    copies = [pltpu.make_async_copy(elem_ref.at[0, m, part], elem.at[m], sems.at[m]) for m in range(elem.shape[0])]
    for copy in copies:
        copy.start()
    for m, copy in enumerate(copies):
        copy.wait()
        for h in range(2):
            message[:, (2 * m + h) * 128 : (2 * m + h + 1) * 128] = elem[m, h * 64 : h * 64 + 64, :]


def laid(elemental, after):
    moms, ev = elemental.shape[1], elemental.shape[3]
    return pl.pallas_call(
        lay_kernel,
        out_shape=jax.ShapeDtypeStruct((64, 2 * moms * ev), bf16),
        in_specs=[pl.BlockSpec(memory_space=pl.ANY)] * 2,
        out_specs=pl.BlockSpec(memory_space=pltpu.VMEM),
        scratch_shapes=[pltpu.VMEM((moms, ev, ev), bf16), pltpu.SemaphoreType.DMA((moms,))],
        compiler_params=pltpu.CompilerParams(vmem_limit_bytes=LIMIT),
        name="laid",
    )(after, elemental)


def fetch_kernel(mom_ref, gamma_ref, prop_ref, *refs):
    *props, picks, sems = refs
    copies = [pltpu.make_async_copy(prop_ref.at[0, slot], prop, sems.at[slot]) for slot, prop in enumerate(props)]
    for copy in copies:
        copy.start()
    for o in range(mom_ref.shape[0]):
        code = jnp.int32(0)
        for g in range(16):
            code = jnp.where(gamma_ref[o] == g, jnp.int32(CODES[g]), code)
        picks[0, o] = mom_ref[o]
        picks[1, o] = code
    for copy in copies:
        copy.wait()


def fetch(op_mom, op_gamma, prop_src):
    slots, parts, rows, width = prop_src.shape[1:]
    ops = op_mom.shape[0]
    vmem_spec = pl.BlockSpec(memory_space=pltpu.VMEM)
    smem_spec = pl.BlockSpec(memory_space=pltpu.SMEM)
    return pl.pallas_call(
        fetch_kernel,
        out_shape=[jax.ShapeDtypeStruct((parts, rows, width), bf16)] * slots + [jax.ShapeDtypeStruct((2, ops), jnp.int32)],
        in_specs=[smem_spec, smem_spec, pl.BlockSpec(memory_space=pltpu.HBM)],
        out_specs=[vmem_spec] * slots + [smem_spec],
        scratch_shapes=[pltpu.SemaphoreType.DMA((slots,))],
        compiler_params=pltpu.CompilerParams(vmem_limit_bytes=LIMIT),
        name="fetch",
    )(op_mom, op_gamma, prop_src)


def joined(refs):
    return jnp.concatenate([ref[...] for ref in refs], axis=0)


def mixed_kernel(picks, mine_ref, *refs):
    *others, prop, mixed, spins, chosen, chosen_sem = refs
    fetched = pltpu.make_async_copy(picks, chosen, chosen_sem)
    fetched.start()
    moms = spins.shape[0]
    width = prop.shape[2]
    real_first = lax.axis_index("mom") == 0

    def elementals(rows, m):
        return jnp.concatenate([rows[:, (2 * m + h) * 128 : (2 * m + h + 1) * 128] for h in range(2)], axis=0)

    mine = mine_ref[width : width + 64, :]
    other = joined(others)[width : width + 64, :]

    lefts = []
    for m in range(moms):
        one, two = elementals(mine, m), elementals(other, m)
        phi_real = jnp.where(real_first, one, two)
        phi_imag = jnp.where(real_first, two, one)
        lefts.append(jnp.concatenate([phi_real, -phi_imag], axis=1))
        lefts.append(jnp.concatenate([phi_imag, phi_real], axis=1))
    left = jnp.concatenate(lefts, axis=0)
    for s in range(4):
        right = jnp.concatenate([prop[0, s * 128 : s * 128 + 128, :], prop[1, s * 128 : s * 128 + 128, :]], axis=0)
        both = jnp.dot(left, right, preferred_element_type=f32).astype(bf16)
        for m in range(moms):
            real = both[m * 256 : m * 256 + 128]
            imag = both[m * 256 + 128 : m * 256 + 256]
            spins[m, 0, s] = real
            spins[m, 1, s] = -imag
            spins[m, 2, s] = -real
            spins[m, 3, s] = imag

    fetched.wait()
    for o in range(mixed.shape[0]):
        mom = chosen[0, o]
        code = chosen[1, o]
        flip = code & 3
        for s in range(4):
            power = code >> (2 + 2 * s)
            for form, turn in enumerate((0, 3)):
                mixed[o, form, s * 128 : s * 128 + 128, :] = spins[mom, (power + turn) & 3, s ^ flip]


def mixed_blocks(picks, mine, other, prop):
    parts, rows, width = prop.shape
    ops = picks.shape[1]
    moms = 2
    vmem_spec = pl.BlockSpec(memory_space=pltpu.VMEM)
    return pl.pallas_call(
        mixed_kernel,
        out_shape=jax.ShapeDtypeStruct((ops, 2, rows, width), bf16),
        in_specs=[pl.BlockSpec(memory_space=pl.ANY)] + [vmem_spec] * (2 + len(other)),
        out_specs=vmem_spec,
        scratch_shapes=[
            pltpu.VMEM((moms, 4, 4, 128, width), bf16),
            pltpu.SMEM((2, ops), jnp.int32),
            pltpu.SemaphoreType.DMA,
        ],
        compiler_params=pltpu.CompilerParams(vmem_limit_bytes=LIMIT),
        cost_estimate=pl.CostEstimate(flops=1, bytes_accessed=1, transcendentals=0),
        name="mixed",
    )(picks, mine, *other, prop)


def block_kernel(places, cols, counts, *refs):
    groups = []
    for count in counts:
        groups.append(refs[: count + 1])
        refs = refs[count + 1 :]
    mixes = dict(zip(sorted({slot for slot, _ in places}), refs))
    out_ref, made, out_sems = refs[-3:]
    part = lax.axis_index("mom")
    copies = []
    for place, ((slot, hop), (mine, *others)) in enumerate(zip(places, groups)):
        mixed = mixes[slot]
        ops, width = mixed.shape[0], mixed.shape[3]
        source = lax.rem(lax.axis_index("col") + hop, cols)
        ours, theirs = mine[0:width, :], joined(others)[0:width, :]
        sinks = [
            jnp.concatenate([ours, theirs], axis=1),
            jnp.concatenate([jnp.where(part == 0, ours, -ours), jnp.where(part == 0, -theirs, theirs)], axis=1),
        ]
        rows = pl.ds(pl.multiple_of(source * width, width), width)
        for o in range(ops):
            for which in range(2):
                first = part if which == 0 else 1 - part
                right = jnp.concatenate([mixed[o, first], mixed[o, 1 - first]], axis=0)
                made[place, o, which] = jnp.dot(sinks[which], right, preferred_element_type=f32).astype(bf16)
                copies.append(
                    pltpu.make_async_copy(
                        made.at[place, o, which], out_ref.at[0, slot, o, which, rows, :], out_sems.at[place, o, which]
                    )
                )
                copies[-1].start()
    for copy in copies:
        copy.wait()


def blocks(cols, work, mixes, prev, out_shape):
    rows, width = out_shape[4:]
    ops = out_shape[2]
    any_spec = pl.BlockSpec(memory_space=pl.ANY)
    vmem_spec = pl.BlockSpec(memory_space=pltpu.VMEM)
    places = [(slot, hop) for slot, hop, _, _ in work]
    operands = [ref for _, _, mine, others in work for ref in (mine, *others)]
    operands += [mixes[slot] for slot in sorted({slot for slot, _ in places})]
    specs = [vmem_spec] * len(operands)
    aliases = {}
    if prev is not None:
        aliases = {len(operands): 0}
        operands.append(prev)
        specs.append(any_spec)
    return pl.pallas_call(
        functools.partial(block_kernel, places, cols, [len(others) for _, _, _, others in work]),
        out_shape=jax.ShapeDtypeStruct(out_shape, bf16),
        in_specs=specs,
        out_specs=any_spec,
        input_output_aliases=aliases,
        scratch_shapes=[
            pltpu.VMEM((len(places), ops, 2, width, width), bf16),
            pltpu.SemaphoreType.DMA((len(places), ops, 2)),
        ],
        compiler_params=pltpu.CompilerParams(vmem_limit_bytes=LIMIT),
        cost_estimate=pl.CostEstimate(flops=1, bytes_accessed=1, transcendentals=0),
        name="blocks",
    )(*operands)


def signed(block, negative):
    return jnp.where(negative, -block, block)


def half_kernel(mine_ref, mixed, sums):
    part = lax.axis_index("mom")
    for o in range(sums.shape[0]):
        for which in range(2):
            left = mine_ref[...] if which == 0 else signed(mine_ref[...], part == 1)
            first = part if which == 0 else 1 - part
            sums[o, which] = jnp.dot(left, mixed[o, first], preferred_element_type=f32)


def half(mine, mixed):
    ops, width = mixed.shape[0], mixed.shape[3]
    vmem_spec = pl.BlockSpec(memory_space=pltpu.VMEM)
    return pl.pallas_call(
        half_kernel,
        out_shape=jax.ShapeDtypeStruct((ops, 2, width, width), f32),
        in_specs=[vmem_spec] * 2,
        out_specs=vmem_spec,
        compiler_params=pltpu.CompilerParams(vmem_limit_bytes=LIMIT),
        cost_estimate=pl.CostEstimate(flops=1, bytes_accessed=1, transcendentals=0),
        name="half",
    )(mine, mixed)


def rest_kernel(slot, hop, cols, count, *refs):
    others = refs[:count]
    mixed, sums, _, out_ref, made, out_sems = refs[count:]
    ops, width = mixed.shape[0], mixed.shape[3]
    part = lax.axis_index("mom")
    source = lax.rem(lax.axis_index("col") + hop, cols)
    rows = pl.ds(pl.multiple_of(source * width, width), width)
    theirs = joined(others)
    copies = []
    for o in range(ops):
        for which in range(2):
            left = theirs if which == 0 else signed(theirs, part == 0)
            first = part if which == 0 else 1 - part
            block = sums[o, which] + jnp.dot(left, mixed[o, 1 - first], preferred_element_type=f32)
            made[o, which] = block.astype(bf16)
            copies.append(
                pltpu.make_async_copy(made.at[o, which], out_ref.at[0, slot, o, which, rows, :], out_sems.at[o, which])
            )
            copies[-1].start()
    for copy in copies:
        copy.wait()


def rest(slot, hop, cols, others, mixed, sums, prev):
    ops, width = mixed.shape[0], mixed.shape[3]
    any_spec = pl.BlockSpec(memory_space=pl.ANY)
    vmem_spec = pl.BlockSpec(memory_space=pltpu.VMEM)
    return pl.pallas_call(
        functools.partial(rest_kernel, slot, hop, cols, len(others)),
        out_shape=jax.ShapeDtypeStruct(prev.shape, bf16),
        in_specs=[vmem_spec] * (len(others) + 2) + [any_spec],
        out_specs=any_spec,
        input_output_aliases={len(others) + 2: 0},
        scratch_shapes=[pltpu.VMEM((ops, 2, width, width), bf16), pltpu.SemaphoreType.DMA((ops, 2))],
        compiler_params=pltpu.CompilerParams(vmem_limit_bytes=LIMIT),
        cost_estimate=pl.CostEstimate(flops=1, bytes_accessed=1, transcendentals=0),
        name="rest",
    )(*others, mixed, sums, prev)


def on_device(prop_src, prop_sink, elemental, op_mom, op_gamma):
    width = prop_src.shape[4]
    rows = prop_src.shape[3]
    stops = prop_src.shape[1]
    ops = op_mom.shape[0]
    cols = lax.axis_size("col")
    times = lax.axis_size("tm")
    later = [((i + 1) % times, i) for i in range(times)]
    swap = [(0, 1), (1, 0)]
    out_shape = (1, stops, ops, 2, rows, width)
    def swapped(block, pieces):
        cuts = [0, *(block.shape[0] * p // 20 // 16 * 16 for p in pieces), block.shape[0]]
        return [lax.ppermute(block[i:j], "mom", swap) for i, j in zip(cuts, cuts[1:])]

    own = turned(prop_sink)
    moving = [own, laid(elemental, own)]
    out = None
    mixes = {}
    waiting = []
    for slot in range(stops):
        if slot == 0:
            first, second = [lax.ppermute(block, "tm", later) for block in moving]
            *props, picks = fetch(op_mom, op_gamma, prop_src)
            first, props, picks = lax.optimization_barrier((first, props, picks))
            held = jnp.concatenate([first, second])
        else:
            held, out = lax.optimization_barrier((lax.ppermute(held, "tm", later), out))
        other = swapped(held, (6,) if slot == 0 else (6,))
        arrivals = [
            (slot, hop, lax.ppermute(held[:width], "col", [((i + hop) % cols, i) for i in range(cols)]))
            for hop in range(1, cols)
        ]
        mixes[slot] = mixed_blocks(picks, held, other, props[slot])
        out = blocks(cols, waiting + [(slot, 0, held, other)], mixes, out, out_shape)
        waiting = []
        for place, hop, mine in arrivals:
            if slot == stops - 1:
                mine, out = lax.optimization_barrier((mine, out))
            waiting.append((place, hop, mine, swapped(mine, (5,) if slot == 0 else ())))
    for slot, hop, mine, others in waiting:
        out = rest(slot, hop, cols, others, mixes[slot], half(mine, mixes[slot]), out)
    return out


def solution(mesh):
    return jax.shard_map(
        on_device,
        mesh=mesh,
        in_specs=(
            P(("cfg", "tm"), None, None, None, "col"),
            P(("cfg", "tm"), None, None, "col"),
            P(("cfg", "tm"), None, None, None, None),
            P("mom"),
            P("mom"),
        ),
        out_specs=P(("cfg", "tm"), None, "mom", None, None, "col"),
        check_vma=False,
    )
```

```python
import functools

import jax
import jax.numpy as jnp
import numpy as np
from jax import lax
from jax.experimental import pallas as pl
from jax.experimental.pallas import tpu as pltpu
from jax.sharding import PartitionSpec as P

bf16 = jnp.bfloat16
f32 = jnp.float32
LIMIT = 16 * 2**20


def gamma_codes():
    one = np.array([[0, 0, 0, 1j], [0, 0, 1j, 0], [0, -1j, 0, 0], [-1j, 0, 0, 0]])
    two = np.array([[0, 0, 0, -1], [0, 0, 1, 0], [0, 1, 0, 0], [-1, 0, 0, 0]], dtype=complex)
    three = np.array([[0, 0, 1j, 0], [0, 0, 0, -1j], [-1j, 0, 0, 0], [0, 1j, 0, 0]])
    four = np.array([[0, 0, 1, 0], [0, 0, 0, 1], [1, 0, 0, 0], [0, 1, 0, 0]], dtype=complex)
    codes = []
    for number in range(16):
        product = np.eye(4, dtype=complex)
        for position, factor in enumerate((one, two, three, four)):
            if number >> position & 1:
                product = product @ factor
        flip = int(np.nonzero(product[0])[0][0])
        code = flip
        for s in range(4):
            assert np.count_nonzero(product[s]) == 1
            power = [p for p in range(4) if product[s, s ^ flip] == (1, 1j, -1, -1j)[p]]
            code |= power[0] << (2 + 2 * s)
        codes.append(code)
    return codes


CODES = gamma_codes()


def turn_kernel(sink_ref, message, sink, sem):
    first = pltpu.make_async_copy(sink_ref.at[0, lax.axis_index("mom")], sink, sem)
    first.start()
    first.wait()
    message[...] = sink[...].T


def turned(prop_sink):
    rows, columns = prop_sink.shape[2:]
    return pl.pallas_call(
        turn_kernel,
        out_shape=jax.ShapeDtypeStruct((columns, rows), bf16),
        in_specs=[pl.BlockSpec(memory_space=pl.ANY)],
        out_specs=pl.BlockSpec(memory_space=pltpu.VMEM),
        scratch_shapes=[pltpu.VMEM((rows, columns), bf16), pltpu.SemaphoreType.DMA],
        compiler_params=pltpu.CompilerParams(vmem_limit_bytes=LIMIT),
        name="turned",
    )(prop_sink)


def lay_kernel(after_ref, elem_ref, message, elem, sems):
    del after_ref
    part = lax.axis_index("mom")
    copies = [pltpu.make_async_copy(elem_ref.at[0, m, part], elem.at[m], sems.at[m]) for m in range(elem.shape[0])]
    for copy in copies:
        copy.start()
    for m, copy in enumerate(copies):
        copy.wait()
        for h in range(2):
            message[:, (2 * m + h) * 128 : (2 * m + h + 1) * 128] = elem[m, h * 64 : h * 64 + 64, :]


def laid(elemental, after):
    moms, ev = elemental.shape[1], elemental.shape[3]
    return pl.pallas_call(
        lay_kernel,
        out_shape=jax.ShapeDtypeStruct((64, 2 * moms * ev), bf16),
        in_specs=[pl.BlockSpec(memory_space=pl.ANY)] * 2,
        out_specs=pl.BlockSpec(memory_space=pltpu.VMEM),
        scratch_shapes=[pltpu.VMEM((moms, ev, ev), bf16), pltpu.SemaphoreType.DMA((moms,))],
        compiler_params=pltpu.CompilerParams(vmem_limit_bytes=LIMIT),
        name="laid",
    )(after, elemental)


def fetch_kernel(mom_ref, gamma_ref, prop_ref, *refs):
    *props, picks, sems = refs
    copies = [pltpu.make_async_copy(prop_ref.at[0, slot], prop, sems.at[slot]) for slot, prop in enumerate(props)]
    for copy in copies:
        copy.start()
    for o in range(mom_ref.shape[0]):
        code = jnp.int32(0)
        for g in range(16):
            code = jnp.where(gamma_ref[o] == g, jnp.int32(CODES[g]), code)
        picks[0, o] = mom_ref[o]
        picks[1, o] = code
    for copy in copies:
        copy.wait()


def fetch(op_mom, op_gamma, prop_src):
    slots, parts, rows, width = prop_src.shape[1:]
    ops = op_mom.shape[0]
    vmem_spec = pl.BlockSpec(memory_space=pltpu.VMEM)
    smem_spec = pl.BlockSpec(memory_space=pltpu.SMEM)
    return pl.pallas_call(
        fetch_kernel,
        out_shape=[jax.ShapeDtypeStruct((parts, rows, width), bf16)] * slots + [jax.ShapeDtypeStruct((2, ops), jnp.int32)],
        in_specs=[smem_spec, smem_spec, pl.BlockSpec(memory_space=pltpu.HBM)],
        out_specs=[vmem_spec] * slots + [smem_spec],
        scratch_shapes=[pltpu.SemaphoreType.DMA((slots,))],
        compiler_params=pltpu.CompilerParams(vmem_limit_bytes=LIMIT),
        name="fetch",
    )(op_mom, op_gamma, prop_src)


def joined(refs):
    return jnp.concatenate([ref[...] for ref in refs], axis=0)


def mixed_kernel(picks, mine_ref, *refs):
    first, prop, mixed, spins, chosen, chosen_sem = refs
    fetched = pltpu.make_async_copy(picks, chosen, chosen_sem)
    fetched.start()
    moms = spins.shape[0]
    width = prop.shape[2]
    real_first = lax.axis_index("mom") == 0

    def elementals(rows, m):
        return jnp.concatenate([rows[:, (2 * m + h) * 128 : (2 * m + h + 1) * 128] for h in range(2)], axis=0)

    mine = mine_ref[0:64, :]
    other = first[0:64, :]

    lefts = []
    for m in range(moms):
        one, two = elementals(mine, m), elementals(other, m)
        phi_real = jnp.where(real_first, one, two)
        phi_imag = jnp.where(real_first, two, one)
        lefts.append(jnp.concatenate([phi_real, -phi_imag], axis=1))
        lefts.append(jnp.concatenate([phi_imag, phi_real], axis=1))
    left = jnp.concatenate(lefts, axis=0)
    for s in range(4):
        right = jnp.concatenate([prop[0, s * 128 : s * 128 + 128, :], prop[1, s * 128 : s * 128 + 128, :]], axis=0)
        both = jnp.dot(left, right, preferred_element_type=f32).astype(bf16)
        for m in range(moms):
            real = both[m * 256 : m * 256 + 128]
            imag = both[m * 256 + 128 : m * 256 + 256]
            spins[m, 0, s] = real
            spins[m, 1, s] = -imag
            spins[m, 2, s] = -real
            spins[m, 3, s] = imag

    fetched.wait()
    for o in range(mixed.shape[0]):
        mom = chosen[0, o]
        code = chosen[1, o]
        flip = code & 3
        for s in range(4):
            power = code >> (2 + 2 * s)
            for form, turn in enumerate((0, 3)):
                mixed[o, form, s * 128 : s * 128 + 128, :] = spins[mom, (power + turn) & 3, s ^ flip]


def mixed_blocks(picks, mine, other, prop):
    parts, rows, width = prop.shape
    ops = picks.shape[1]
    moms = 2
    vmem_spec = pl.BlockSpec(memory_space=pltpu.VMEM)
    return pl.pallas_call(
        mixed_kernel,
        out_shape=jax.ShapeDtypeStruct((ops, 2, rows, width), bf16),
        in_specs=[pl.BlockSpec(memory_space=pl.ANY)] + [vmem_spec] * 3,
        out_specs=vmem_spec,
        scratch_shapes=[
            pltpu.VMEM((moms, 4, 4, 128, width), bf16),
            pltpu.SMEM((2, ops), jnp.int32),
            pltpu.SemaphoreType.DMA,
        ],
        compiler_params=pltpu.CompilerParams(vmem_limit_bytes=LIMIT),
        cost_estimate=pl.CostEstimate(flops=1, bytes_accessed=1, transcendentals=0),
        name="mixed",
    )(picks, mine, other, prop)


def block_kernel(places, cols, counts, *refs):
    groups = []
    for count in counts:
        groups.append(refs[: count + 1])
        refs = refs[count + 1 :]
    mixes = dict(zip(sorted({slot for slot, _ in places}), refs))
    out_ref, made, out_sems = refs[-3:]
    part = lax.axis_index("mom")
    copies = []
    for place, ((slot, hop), (mine, *others)) in enumerate(zip(places, groups)):
        mixed = mixes[slot]
        ops, width = mixed.shape[0], mixed.shape[3]
        source = lax.rem(lax.axis_index("col") + hop, cols)
        ours, theirs = mine[mine.shape[0] - width :, :], joined(others)[-width:, :]
        sinks = [
            jnp.concatenate([ours, theirs], axis=1),
            jnp.concatenate([jnp.where(part == 0, ours, -ours), jnp.where(part == 0, -theirs, theirs)], axis=1),
        ]
        rows = pl.ds(pl.multiple_of(source * width, width), width)
        for o in range(ops):
            for which in range(2):
                first = part if which == 0 else 1 - part
                right = jnp.concatenate([mixed[o, first], mixed[o, 1 - first]], axis=0)
                made[place, o, which] = jnp.dot(sinks[which], right, preferred_element_type=f32).astype(bf16)
                copies.append(
                    pltpu.make_async_copy(
                        made.at[place, o, which], out_ref.at[0, slot, o, which, rows, :], out_sems.at[place, o, which]
                    )
                )
                copies[-1].start()
    for copy in copies:
        copy.wait()


def blocks(cols, work, mixes, prev, out_shape):
    rows, width = out_shape[4:]
    ops = out_shape[2]
    any_spec = pl.BlockSpec(memory_space=pl.ANY)
    vmem_spec = pl.BlockSpec(memory_space=pltpu.VMEM)
    places = [(slot, hop) for slot, hop, _, _ in work]
    operands = [ref for _, _, mine, others in work for ref in (mine, *others)]
    operands += [mixes[slot] for slot in sorted({slot for slot, _ in places})]
    specs = [vmem_spec] * len(operands)
    aliases = {}
    if prev is not None:
        aliases = {len(operands): 0}
        operands.append(prev)
        specs.append(any_spec)
    return pl.pallas_call(
        functools.partial(block_kernel, places, cols, [len(others) for _, _, _, others in work]),
        out_shape=jax.ShapeDtypeStruct(out_shape, bf16),
        in_specs=specs,
        out_specs=any_spec,
        input_output_aliases=aliases,
        scratch_shapes=[
            pltpu.VMEM((len(places), ops, 2, width, width), bf16),
            pltpu.SemaphoreType.DMA((len(places), ops, 2)),
        ],
        compiler_params=pltpu.CompilerParams(vmem_limit_bytes=LIMIT),
        cost_estimate=pl.CostEstimate(flops=1, bytes_accessed=1, transcendentals=0),
        name="blocks",
    )(*operands)


def signed(block, negative):
    return jnp.where(negative, -block, block)


def half_kernel(mine_ref, mixed, sums):
    part = lax.axis_index("mom")
    for o in range(sums.shape[0]):
        for which in range(2):
            left = mine_ref[...] if which == 0 else signed(mine_ref[...], part == 1)
            first = part if which == 0 else 1 - part
            sums[o, which] = jnp.dot(left, mixed[o, first], preferred_element_type=f32)


def half(mine, mixed):
    ops, width = mixed.shape[0], mixed.shape[3]
    vmem_spec = pl.BlockSpec(memory_space=pltpu.VMEM)
    return pl.pallas_call(
        half_kernel,
        out_shape=jax.ShapeDtypeStruct((ops, 2, width, width), f32),
        in_specs=[vmem_spec] * 2,
        out_specs=vmem_spec,
        compiler_params=pltpu.CompilerParams(vmem_limit_bytes=LIMIT),
        cost_estimate=pl.CostEstimate(flops=1, bytes_accessed=1, transcendentals=0),
        name="half",
    )(mine, mixed)


def rest_kernel(slot, hop, cols, count, *refs):
    others = refs[:count]
    mixed, sums, _, out_ref, made, out_sems = refs[count:]
    ops, width = mixed.shape[0], mixed.shape[3]
    part = lax.axis_index("mom")
    source = lax.rem(lax.axis_index("col") + hop, cols)
    rows = pl.ds(pl.multiple_of(source * width, width), width)
    theirs = joined(others)
    copies = []
    for o in range(ops):
        for which in range(2):
            left = theirs if which == 0 else signed(theirs, part == 0)
            first = part if which == 0 else 1 - part
            block = sums[o, which] + jnp.dot(left, mixed[o, 1 - first], preferred_element_type=f32)
            made[o, which] = block.astype(bf16)
            copies.append(
                pltpu.make_async_copy(made.at[o, which], out_ref.at[0, slot, o, which, rows, :], out_sems.at[o, which])
            )
            copies[-1].start()
    for copy in copies:
        copy.wait()


def rest(slot, hop, cols, others, mixed, sums, prev):
    ops, width = mixed.shape[0], mixed.shape[3]
    any_spec = pl.BlockSpec(memory_space=pl.ANY)
    vmem_spec = pl.BlockSpec(memory_space=pltpu.VMEM)
    return pl.pallas_call(
        functools.partial(rest_kernel, slot, hop, cols, len(others)),
        out_shape=jax.ShapeDtypeStruct(prev.shape, bf16),
        in_specs=[vmem_spec] * (len(others) + 2) + [any_spec],
        out_specs=any_spec,
        input_output_aliases={len(others) + 2: 0},
        scratch_shapes=[pltpu.VMEM((ops, 2, width, width), bf16), pltpu.SemaphoreType.DMA((ops, 2))],
        compiler_params=pltpu.CompilerParams(vmem_limit_bytes=LIMIT),
        cost_estimate=pl.CostEstimate(flops=1, bytes_accessed=1, transcendentals=0),
        name="rest",
    )(*others, mixed, sums, prev)


def on_device(prop_src, prop_sink, elemental, op_mom, op_gamma):
    width = prop_src.shape[4]
    rows = prop_src.shape[3]
    stops = prop_src.shape[1]
    ops = op_mom.shape[0]
    cols = lax.axis_size("col")
    times = lax.axis_size("tm")
    later = [((i + 1) % times, i) for i in range(times)]
    swap = [(0, 1), (1, 0)]
    out_shape = (1, stops, ops, 2, rows, width)
    def swapped(block, pieces):
        cuts = [0, *(block.shape[0] * p // 20 // 16 * 16 for p in pieces), block.shape[0]]
        return [lax.ppermute(block[i:j], "mom", swap) for i, j in zip(cuts, cuts[1:])]

    own = turned(prop_sink)
    moving = [own, laid(elemental, own)]
    out = None
    mixes = {}
    waiting = []
    for slot in range(stops):
        if slot == 0:
            first, second = [lax.ppermute(block, "tm", later) for block in moving]
            *props, picks = fetch(op_mom, op_gamma, prop_src)
            first, props, picks = lax.optimization_barrier((first, props, picks))
            held = jnp.concatenate([second, first])
        else:
            held, out = lax.optimization_barrier((lax.ppermute(held, "tm", later), out))
        other = swapped(held, (10,) if slot == 0 else (14,))
        arrivals = [
            (slot, hop, lax.ppermute(held[-width:], "col", [((i + hop) % cols, i) for i in range(cols)]))
            for hop in range(1, cols)
        ]
        mixes[slot] = mixed_blocks(picks, held, other[0], props[slot])
        out = blocks(cols, waiting + [(slot, 0, held, other)], mixes, out, out_shape)
        waiting = []
        for place, hop, mine in arrivals:
            if slot == stops - 1:
                mine, out = lax.optimization_barrier((mine, out))
            waiting.append((place, hop, mine, swapped(mine, (5,) if slot == 0 else ())))
    for slot, hop, mine, others in waiting:
        out = rest(slot, hop, cols, others, mixes[slot], half(mine, mixes[slot]), out)
    return out


def solution(mesh):
    return jax.shard_map(
        on_device,
        mesh=mesh,
        in_specs=(
            P(("cfg", "tm"), None, None, None, "col"),
            P(("cfg", "tm"), None, None, "col"),
            P(("cfg", "tm"), None, None, None, None),
            P("mom"),
            P("mom"),
        ),
        out_specs=P(("cfg", "tm"), None, "mom", None, None, "col"),
        check_vma=False,
    )
```

```python
import functools

import jax
import jax.numpy as jnp
import numpy as np
from jax import lax
from jax.experimental import pallas as pl
from jax.experimental.pallas import tpu as pltpu
from jax.sharding import PartitionSpec as P

bf16 = jnp.bfloat16
f32 = jnp.float32
LIMIT = 16 * 2**20


def gamma_codes():
    one = np.array([[0, 0, 0, 1j], [0, 0, 1j, 0], [0, -1j, 0, 0], [-1j, 0, 0, 0]])
    two = np.array([[0, 0, 0, -1], [0, 0, 1, 0], [0, 1, 0, 0], [-1, 0, 0, 0]], dtype=complex)
    three = np.array([[0, 0, 1j, 0], [0, 0, 0, -1j], [-1j, 0, 0, 0], [0, 1j, 0, 0]])
    four = np.array([[0, 0, 1, 0], [0, 0, 0, 1], [1, 0, 0, 0], [0, 1, 0, 0]], dtype=complex)
    codes = []
    for number in range(16):
        product = np.eye(4, dtype=complex)
        for position, factor in enumerate((one, two, three, four)):
            if number >> position & 1:
                product = product @ factor
        flip = int(np.nonzero(product[0])[0][0])
        code = flip
        for s in range(4):
            assert np.count_nonzero(product[s]) == 1
            power = [p for p in range(4) if product[s, s ^ flip] == (1, 1j, -1, -1j)[p]]
            code |= power[0] << (2 + 2 * s)
        codes.append(code)
    return codes


CODES = gamma_codes()


def turn_kernel(sink_ref, message, sink, sem):
    first = pltpu.make_async_copy(sink_ref.at[0, lax.axis_index("mom")], sink, sem)
    first.start()
    first.wait()
    message[...] = sink[...].T


def turned(prop_sink):
    rows, columns = prop_sink.shape[2:]
    return pl.pallas_call(
        turn_kernel,
        out_shape=jax.ShapeDtypeStruct((columns, rows), bf16),
        in_specs=[pl.BlockSpec(memory_space=pl.ANY)],
        out_specs=pl.BlockSpec(memory_space=pltpu.VMEM),
        scratch_shapes=[pltpu.VMEM((rows, columns), bf16), pltpu.SemaphoreType.DMA],
        compiler_params=pltpu.CompilerParams(vmem_limit_bytes=107 * 2**19),
        name="turned",
    )(prop_sink)


def lay_kernel(after_ref, elem_ref, message, elem, sems):
    del after_ref
    part = lax.axis_index("mom")
    copies = [pltpu.make_async_copy(elem_ref.at[0, m, part], elem.at[m], sems.at[m]) for m in range(elem.shape[0])]
    for copy in copies:
        copy.start()
    for m, copy in enumerate(copies):
        copy.wait()
        for h in range(2):
            message[:, (2 * m + h) * 128 : (2 * m + h + 1) * 128] = elem[m, h * 64 : h * 64 + 64, :]


def laid(elemental, after):
    moms, ev = elemental.shape[1], elemental.shape[3]
    return pl.pallas_call(
        lay_kernel,
        out_shape=jax.ShapeDtypeStruct((64, 2 * moms * ev), bf16),
        in_specs=[pl.BlockSpec(memory_space=pl.ANY)] * 2,
        out_specs=pl.BlockSpec(memory_space=pltpu.VMEM),
        scratch_shapes=[pltpu.VMEM((moms, ev, ev), bf16), pltpu.SemaphoreType.DMA((moms,))],
        compiler_params=pltpu.CompilerParams(vmem_limit_bytes=LIMIT),
        name="laid",
    )(after, elemental)


def fetch_kernel(mom_ref, gamma_ref, prop_ref, *refs):
    *props, picks, sems = refs
    copies = [pltpu.make_async_copy(prop_ref.at[0, slot], prop, sems.at[slot]) for slot, prop in enumerate(props)]
    for copy in copies:
        copy.start()
    for o in range(mom_ref.shape[0]):
        code = jnp.int32(0)
        for g in range(16):
            code = jnp.where(gamma_ref[o] == g, jnp.int32(CODES[g]), code)
        picks[0, o] = mom_ref[o]
        picks[1, o] = code
    for copy in copies:
        copy.wait()


def fetch(op_mom, op_gamma, prop_src):
    slots, parts, rows, width = prop_src.shape[1:]
    ops = op_mom.shape[0]
    vmem_spec = pl.BlockSpec(memory_space=pltpu.VMEM)
    smem_spec = pl.BlockSpec(memory_space=pltpu.SMEM)
    return pl.pallas_call(
        fetch_kernel,
        out_shape=[jax.ShapeDtypeStruct((parts, rows, width), bf16)] * slots + [jax.ShapeDtypeStruct((2, ops), jnp.int32)],
        in_specs=[smem_spec, smem_spec, pl.BlockSpec(memory_space=pltpu.HBM)],
        out_specs=[vmem_spec] * slots + [smem_spec],
        scratch_shapes=[pltpu.SemaphoreType.DMA((slots,))],
        compiler_params=pltpu.CompilerParams(vmem_limit_bytes=LIMIT),
        name="fetch",
    )(op_mom, op_gamma, prop_src)


def joined(refs):
    return jnp.concatenate([ref[...] for ref in refs], axis=0)


def mixed_kernel(picks, mine_ref, *refs):
    first, prop, mixed, spins, chosen, chosen_sem = refs
    fetched = pltpu.make_async_copy(picks, chosen, chosen_sem)
    fetched.start()
    moms = spins.shape[0]
    width = prop.shape[2]
    real_first = lax.axis_index("mom") == 0

    def elementals(rows, m):
        return jnp.concatenate([rows[:, (2 * m + h) * 128 : (2 * m + h + 1) * 128] for h in range(2)], axis=0)

    mine = mine_ref[0:64, :]
    other = first[0:64, :]

    lefts = []
    for m in range(moms):
        one, two = elementals(mine, m), elementals(other, m)
        phi_real = jnp.where(real_first, one, two)
        phi_imag = jnp.where(real_first, two, one)
        lefts.append(jnp.concatenate([phi_real, -phi_imag], axis=1))
        lefts.append(jnp.concatenate([phi_imag, phi_real], axis=1))
    left = jnp.concatenate(lefts, axis=0)
    for s in range(4):
        right = jnp.concatenate([prop[0, s * 128 : s * 128 + 128, :], prop[1, s * 128 : s * 128 + 128, :]], axis=0)
        both = jnp.dot(left, right, preferred_element_type=f32).astype(bf16)
        for m in range(moms):
            real = both[m * 256 : m * 256 + 128]
            imag = both[m * 256 + 128 : m * 256 + 256]
            spins[m, 0, s] = real
            spins[m, 1, s] = -imag
            spins[m, 2, s] = -real
            spins[m, 3, s] = imag

    fetched.wait()
    for o in range(mixed.shape[0]):
        mom = chosen[0, o]
        code = chosen[1, o]
        flip = code & 3
        for s in range(4):
            power = code >> (2 + 2 * s)
            for form, turn in enumerate((0, 3)):
                mixed[o, form, s * 128 : s * 128 + 128, :] = spins[mom, (power + turn) & 3, s ^ flip]


def mixed_blocks(picks, mine, other, prop):
    parts, rows, width = prop.shape
    ops = picks.shape[1]
    moms = 2
    vmem_spec = pl.BlockSpec(memory_space=pltpu.VMEM)
    return pl.pallas_call(
        mixed_kernel,
        out_shape=jax.ShapeDtypeStruct((ops, 2, rows, width), bf16),
        in_specs=[pl.BlockSpec(memory_space=pl.ANY)] + [vmem_spec] * 3,
        out_specs=vmem_spec,
        scratch_shapes=[
            pltpu.VMEM((moms, 4, 4, 128, width), bf16),
            pltpu.SMEM((2, ops), jnp.int32),
            pltpu.SemaphoreType.DMA,
        ],
        compiler_params=pltpu.CompilerParams(vmem_limit_bytes=LIMIT),
        cost_estimate=pl.CostEstimate(flops=1, bytes_accessed=1, transcendentals=0),
        name="mixed",
    )(picks, mine, other, prop)


def block_kernel(places, cols, counts, *refs):
    groups = []
    for count in counts:
        groups.append(refs[: count + 1])
        refs = refs[count + 1 :]
    mixes = dict(zip(sorted({slot for slot, _ in places}), refs))
    out_ref, made, out_sems = refs[-3:]
    part = lax.axis_index("mom")
    copies = []
    for place, ((slot, hop), (mine, *others)) in enumerate(zip(places, groups)):
        mixed = mixes[slot]
        ops, width = mixed.shape[0], mixed.shape[3]
        source = lax.rem(lax.axis_index("col") + hop, cols)
        ours, theirs = mine[mine.shape[0] - width :, :], joined(others)[-width:, :]
        sinks = [
            jnp.concatenate([ours, theirs], axis=1),
            jnp.concatenate([jnp.where(part == 0, ours, -ours), jnp.where(part == 0, -theirs, theirs)], axis=1),
        ]
        rows = pl.ds(pl.multiple_of(source * width, width), width)
        for o in range(ops):
            for which in range(2):
                first = part if which == 0 else 1 - part
                right = jnp.concatenate([mixed[o, first], mixed[o, 1 - first]], axis=0)
                made[place, o, which] = jnp.dot(sinks[which], right, preferred_element_type=f32).astype(bf16)
                copies.append(
                    pltpu.make_async_copy(
                        made.at[place, o, which], out_ref.at[0, slot, o, which, rows, :], out_sems.at[place, o, which]
                    )
                )
                copies[-1].start()
    for copy in copies:
        copy.wait()


def blocks(cols, work, mixes, prev, out_shape):
    rows, width = out_shape[4:]
    ops = out_shape[2]
    any_spec = pl.BlockSpec(memory_space=pl.ANY)
    vmem_spec = pl.BlockSpec(memory_space=pltpu.VMEM)
    places = [(slot, hop) for slot, hop, _, _ in work]
    operands = [ref for _, _, mine, others in work for ref in (mine, *others)]
    operands += [mixes[slot] for slot in sorted({slot for slot, _ in places})]
    specs = [vmem_spec] * len(operands)
    aliases = {}
    if prev is not None:
        aliases = {len(operands): 0}
        operands.append(prev)
        specs.append(any_spec)
    return pl.pallas_call(
        functools.partial(block_kernel, places, cols, [len(others) for _, _, _, others in work]),
        out_shape=jax.ShapeDtypeStruct(out_shape, bf16),
        in_specs=specs,
        out_specs=any_spec,
        input_output_aliases=aliases,
        scratch_shapes=[
            pltpu.VMEM((len(places), ops, 2, width, width), bf16),
            pltpu.SemaphoreType.DMA((len(places), ops, 2)),
        ],
        compiler_params=pltpu.CompilerParams(vmem_limit_bytes=LIMIT),
        cost_estimate=pl.CostEstimate(flops=1, bytes_accessed=1, transcendentals=0),
        name="blocks",
    )(*operands)


def signed(block, negative):
    return jnp.where(negative, -block, block)


def half_kernel(mine_ref, mixed, sums):
    part = lax.axis_index("mom")
    for o in range(sums.shape[0]):
        for which in range(2):
            left = mine_ref[...] if which == 0 else signed(mine_ref[...], part == 1)
            first = part if which == 0 else 1 - part
            sums[o, which] = jnp.dot(left, mixed[o, first], preferred_element_type=f32)


def half(mine, mixed):
    ops, width = mixed.shape[0], mixed.shape[3]
    vmem_spec = pl.BlockSpec(memory_space=pltpu.VMEM)
    return pl.pallas_call(
        half_kernel,
        out_shape=jax.ShapeDtypeStruct((ops, 2, width, width), f32),
        in_specs=[vmem_spec] * 2,
        out_specs=vmem_spec,
        compiler_params=pltpu.CompilerParams(vmem_limit_bytes=LIMIT),
        cost_estimate=pl.CostEstimate(flops=1, bytes_accessed=1, transcendentals=0),
        name="half",
    )(mine, mixed)


def rest_kernel(slot, hop, cols, count, *refs):
    others = refs[:count]
    mixed, sums, _, out_ref, made, out_sems = refs[count:]
    ops, width = mixed.shape[0], mixed.shape[3]
    part = lax.axis_index("mom")
    source = lax.rem(lax.axis_index("col") + hop, cols)
    rows = pl.ds(pl.multiple_of(source * width, width), width)
    theirs = joined(others)
    copies = []
    for o in range(ops):
        for which in range(2):
            left = theirs if which == 0 else signed(theirs, part == 0)
            first = part if which == 0 else 1 - part
            block = sums[o, which] + jnp.dot(left, mixed[o, 1 - first], preferred_element_type=f32)
            made[o, which] = block.astype(bf16)
            copies.append(
                pltpu.make_async_copy(made.at[o, which], out_ref.at[0, slot, o, which, rows, :], out_sems.at[o, which])
            )
            copies[-1].start()
    for copy in copies:
        copy.wait()


def rest(slot, hop, cols, others, mixed, sums, prev):
    ops, width = mixed.shape[0], mixed.shape[3]
    any_spec = pl.BlockSpec(memory_space=pl.ANY)
    vmem_spec = pl.BlockSpec(memory_space=pltpu.VMEM)
    return pl.pallas_call(
        functools.partial(rest_kernel, slot, hop, cols, len(others)),
        out_shape=jax.ShapeDtypeStruct(prev.shape, bf16),
        in_specs=[vmem_spec] * (len(others) + 2) + [any_spec],
        out_specs=any_spec,
        input_output_aliases={len(others) + 2: 0},
        scratch_shapes=[pltpu.VMEM((ops, 2, width, width), bf16), pltpu.SemaphoreType.DMA((ops, 2))],
        compiler_params=pltpu.CompilerParams(vmem_limit_bytes=LIMIT),
        cost_estimate=pl.CostEstimate(flops=1, bytes_accessed=1, transcendentals=0),
        name="rest",
    )(*others, mixed, sums, prev)


def on_device(prop_src, prop_sink, elemental, op_mom, op_gamma):
    width = prop_src.shape[4]
    rows = prop_src.shape[3]
    stops = prop_src.shape[1]
    ops = op_mom.shape[0]
    cols = lax.axis_size("col")
    times = lax.axis_size("tm")
    later = [((i + 1) % times, i) for i in range(times)]
    swap = [(0, 1), (1, 0)]
    out_shape = (1, stops, ops, 2, rows, width)
    def swapped(block, pieces):
        cuts = [0, *(block.shape[0] * p // 20 // 16 * 16 for p in pieces), block.shape[0]]
        return [lax.ppermute(block[i:j], "mom", swap) for i, j in zip(cuts, cuts[1:])]

    own = turned(prop_sink)
    moving = [own, laid(elemental, own)]
    out = None
    mixes = {}
    waiting = []
    for slot in range(stops):
        if slot == 0:
            first, second = [lax.ppermute(block, "tm", later) for block in moving]
            *props, picks = fetch(op_mom, op_gamma, prop_src)
            first, props, picks = lax.optimization_barrier((first, props, picks))
            held = jnp.concatenate([second, first])
        else:
            held, out = lax.optimization_barrier((lax.ppermute(held, "tm", later), out))
        other = swapped(held, (10,) if slot == 0 else (14,))
        arrivals = [
            (slot, hop, lax.ppermute(held[-width:], "col", [((i + hop) % cols, i) for i in range(cols)]))
            for hop in range(1, cols)
        ]
        mixes[slot] = mixed_blocks(picks, held, other[0], props[slot])
        out = blocks(cols, waiting + [(slot, 0, held, other)], mixes, out, out_shape)
        waiting = []
        for place, hop, mine in arrivals:
            if slot == stops - 1:
                mine, out = lax.optimization_barrier((mine, out))
            waiting.append((place, hop, mine, swapped(mine, (5,) if slot == 0 else ())))
    for slot, hop, mine, others in waiting:
        out = rest(slot, hop, cols, others, mixes[slot], half(mine, mixes[slot]), out)
    return out


def solution(mesh):
    return jax.shard_map(
        on_device,
        mesh=mesh,
        in_specs=(
            P(("cfg", "tm"), None, None, None, "col"),
            P(("cfg", "tm"), None, None, "col"),
            P(("cfg", "tm"), None, None, None, None),
            P("mom"),
            P("mom"),
        ),
        out_specs=P(("cfg", "tm"), None, "mom", None, None, "col"),
        check_vma=False,
    )
```
